256 devices in a mesh: ctx: 16 (over x, z_hi, core), fsdp: 16 (over y, z_lo).
Axes of the slice: x: 4, y: 4, z: 8 (z_hi: 2, z_lo: 4; z = z_hi * 4 + z_lo), core: 2. Of those that a mesh axis runs over, the one named last changes fastest.
Arguments:
- rows_in: bfloat16 [16, 2048, 12288], P('fsdp', 'ctx'), may hold values from -6 to 6
- cotangent: bfloat16 [16, 2048, 4096], P('fsdp', 'ctx'), may hold values from -6 to 6
- taps: float32 [3, 12288], P(None, 'fsdp'), may hold values from -3 to 3
- residues: float32 [16, 4096], P(None, 'fsdp'), may hold values from -1 to 1, as said below
- rates: float32 [16, 4096], P(None, 'fsdp'), may hold values from 0 to 1, as said below
- skip: float32 [4096], P('fsdp'), may hold values from -3 to 3
- state_before: float32 [16, 16, 4096], P('fsdp'), may hold values from -24 to 24
- adjoint_after: float32 [16, 16, 4096], P('fsdp'), may hold values from -24 to 24
Outputs:
- grad_rows: bfloat16 [16, 2048, 12288], P('fsdp', 'ctx')
- grad_taps: float32 [3, 12288], P(None, 'fsdp')
- grad_residues: float32 [16, 4096], P(None, 'fsdp')
- grad_rates: float32 [16, 4096], P(None, 'fsdp')
- grad_skip: float32 [4096], P('fsdp')
The draws below stay inside these ranges and needn't reach their ends.
Inputs may be any that keep to these rules, and one draw needn't show every extreme that they name: Positive decay rates. Real residues.
All inputs are finite; a program needn't handle non-finite values.
Results may differ from the reference program's by a relative error of at most 0.0011.
Values may be sent and summed in bfloat16 or wider, within the bound.
A program may use at most 128 MiB of HBM per device.

```python
import math
import jax
import jax.numpy as jnp
from jax import lax

C = 4096
M = 16
TOKENS = 2048
SEQS = 16


def rate_values(key, low, high):
    pick = jax.random.uniform(key, (M, C), jnp.float32)
    return jnp.exp(jnp.log(low) + pick * (jnp.log(high) - jnp.log(low)))


def draw_rates(key, part):
    values = rate_values(key, 0.03 / TOKENS, 1.0 / 30.0)
    return values


def draw_residues(key, part):
    values = rate_values(key, 0.03 / TOKENS, 1.0 / 30.0)
    own = jax.random.fold_in(key, 7)
    signed = jax.random.truncated_normal(own, -6.0, 6.0, (M, C), jnp.float32)
    return signed * jnp.sqrt(2.0 * values) * 0.25


def spiked(entries, key, source, target, blocks, factor):
    def block_of(dim):
        return (jnp.arange(entries.shape[dim]) // (entries.shape[dim] // blocks)).reshape((-1,) + (1,) * (entries.ndim - 1 - dim))

    first = jax.random.permutation(key, blocks)[block_of(target)]
    second = (block_of(target) + blocks // 2) % blocks
    return jnp.where((block_of(source) == first) | (block_of(source) == second), factor * entries, entries)


def levels(own_key, shape, pieces, smallest, largest):
    level = 1.0
    for dim, parts in pieces:
        heights = jax.random.uniform(jax.random.fold_in(jax.random.fold_in(own_key, 6), dim), (parts,), jnp.float32, smallest / len(pieces), largest / len(pieces))
        level = level * jnp.repeat(jnp.exp(heights), shape[dim] // parts).reshape((-1,) + (1,) * (len(shape) - 1 - dim))
    return level


def noise(rng, dims, width, reach, pieces=(), dtype=jnp.bfloat16):
    gain = levels(rng, dims, pieces, -0.22, 0.18) if pieces else 1.0
    entries = jax.random.normal(rng, dims, jnp.float32) * width * gain
    return jnp.minimum(jnp.maximum(entries, -reach), reach).astype(dtype)


def gaussian_with(stream_key, extent, spread, most, pieces, heavy, kind=jnp.bfloat16):
    values = spread * jax.random.normal(stream_key, extent, jnp.float32)
    if pieces:
        values = values * levels(stream_key, extent, pieces, -0.22, 0.18)
    return jnp.clip(spiked(values, jax.random.fold_in(stream_key, 3), *heavy), -most, most).astype(kind)


def setup_inputs(seed: int = 0) -> dict:
    seeds = jax.random.split(jax.random.key(seed), 9)
    return {
        "rows_in": noise(seeds[0], (SEQS, TOKENS, 3 * C), 1.0, 6.0, ((0, 16), (1, 16))),
        "cotangent": gaussian_with(seeds[1], (SEQS, TOKENS, C), 1.0, 6.0, ((0, 16), (1, 16)), (1, 2, 16, 2.0)),
        "taps": noise(seeds[2], (3, 3 * C), 0.6, 3.0, ((1, 16),), jnp.float32),
        "residues": draw_residues(jax.random.fold_in(seeds[8], 71), 0),
        "rates": draw_rates(jax.random.fold_in(seeds[8], 71), 0),
        "skip": noise(seeds[5], (C,), 0.5, 3.0, ((0, 16),), jnp.float32),
        "state_before": noise(seeds[6], (SEQS, M, C), 4.0, 24.0, ((0, 16),), jnp.float32),
        "adjoint_after": noise(seeds[7], (SEQS, M, C), 4.0, 24.0, ((0, 16),), jnp.float32),
    }


def featurize(rows, taps):
    one = jnp.concatenate([jnp.zeros_like(rows[:1]), rows[:-1]], 0)
    two = jnp.concatenate([jnp.zeros_like(rows[:2]), rows[:-2]], 0)
    return taps[0] * rows + taps[1] * one + taps[2] * two

def forward(rows, taps, residues, rates, skip, begin):
    feat = featurize(rows, taps)
    query = feat[:, :C]
    keys = feat[:, C:2 * C]
    values = feat[:, 2 * C:]
    mixed = keys * values
    decay = jnp.exp(-rates)

    def advance(state, item):
        state = decay * state + item[None, :]
        return (state, lax.optimization_barrier(jnp.sum(residues * state, 0)))
    final, modal = lax.scan(advance, begin, mixed)
    return (query * (modal + skip * mixed), final)

def reference(rows_in, cotangent, taps, residues, rates, skip, state_before, adjoint_after):
    scale = 1.0 / math.sqrt(SEQS * TOKENS)

    def one_sequence(group):
        rows, cot, begin, ending = group

        def inner(r, t, re, ra, s):
            return forward(r, t, re, ra, s, begin)
        _, pull = jax.vjp(inner, rows.astype(jnp.float32), taps, residues, rates, skip)
        grads = pull((cot.astype(jnp.float32), residues * jnp.exp(-rates) * ending))
        return (grads[0].astype(jnp.bfloat16), grads[1], grads[2], grads[3], grads[4])
    result = lax.map(one_sequence, (rows_in, cotangent, state_before, adjoint_after))
    return (result[0], lax.optimization_barrier(jnp.sum(result[1], 0)) * scale, lax.optimization_barrier(jnp.sum(result[2], 0)) * scale, lax.optimization_barrier(jnp.sum(result[3], 0)) * scale, lax.optimization_barrier(jnp.sum(result[4], 0)) * scale)
```

```python
import math

import jax
import jax.numpy as jnp
from jax import lax
from jax.experimental import pallas as pl
from jax.experimental.pallas import tpu as pltpu
from jax.sharding import PartitionSpec as P

MESH = pl.DeviceIdType.MESH
F32 = jnp.float32
MODES = 16
LANES = 128
STEPS = 16
OWNERS = 16
ROWS = 96
HALF = ROWS // 2
PARTS = 4
PIECE = OWNERS // PARTS
GROUPS = 4
GRID = 32 // GROUPS
VMEM = pl.BlockSpec(memory_space=pltpu.VMEM)


def place():
    p = lax.axis_index("ctx")
    f = lax.axis_index("fsdp")
    return p, f, p % 2, (p // 2) % 2, p // 4


def remote(src, dst, send, recv, ctx, fsdp):
    return pltpu.make_async_remote_copy(
        src_ref=src, dst_ref=dst, send_sem=send, recv_sem=recv,
        device_id=(ctx, fsdp), device_id_type=MESH,
    )


def greet(ctx, fsdp):
    pl.semaphore_signal(
        pltpu.get_barrier_semaphore(), inc=1, device_id=(ctx, fsdp), device_id_type=MESH
    )


def gather_kernel(res, rate, taps, skip, tail, head, gath, prev, nxt, pbuf, nbuf,
                  send, recv, csend, crecv, hsend, hrecv):
    p, f, c, _, _ = place()
    partner = p + 1 - 2 * c
    for step in range(1, OWNERS):
        greet(p, (f + step) % OWNERS)
    outer = (p + 15 + 2 * c) % 16
    greet(partner, f)
    greet(outer, f)

    mine = gath.at[f]
    for b in range(2):
        cols = slice(LANES * b, LANES * (b + 1))
        gath[f, 16 * b : 16 * (b + 1), :] = res[:, cols]
        gath[f, 32 + 16 * b : 48 + 16 * b, :] = rate[:, cols]
        gath[f, 82 + b : 83 + b, :] = skip[:, cols]
    for j in range(3):
        for b in range(6):
            row = 64 + 6 * j + b
            gath[f, row : row + 1, :] = taps[j : j + 1, LANES * b : LANES * (b + 1)]
    gath[f, 84:96, :] = jnp.zeros((12, LANES), F32)
    pl.semaphore_wait(pltpu.get_barrier_semaphore(), OWNERS + 1)

    first = pl.multiple_of(c * HALF, 8)
    own = mine.at[pl.ds(first, HALF)]
    out = []
    for step in range(1, OWNERS):
        to = (f + step) % OWNERS
        copy = remote(own, own, send.at[step], recv.at[step], p, to)
        copy.start()
        out.append(copy)
    right = remote(tail, pbuf, hsend.at[0], hrecv.at[0], p + 1, f)
    left = remote(head, nbuf, hsend.at[1], hrecv.at[1], p - 1, f)

    @pl.when(p < 15)
    def _():
        right.start()

    @pl.when(p > 0)
    def _():
        left.start()

    for step in range(1, OWNERS):
        source = (f + OWNERS - step) % OWNERS
        block = gath.at[source, pl.ds(first, HALF)]
        remote(block, block, send.at[step], recv.at[step], p, f).wait_recv()
        copy = remote(block, block, csend.at[step], crecv.at[step], partner, f)
        copy.start()
        out.append(copy)

    @pl.when(p > 0)
    def _():
        right.wait_recv()
        prev[...] = pbuf[...].astype(F32)

    @pl.when(p == 0)
    def _():
        prev[...] = jnp.zeros_like(prev)

    @pl.when(p < 15)
    def _():
        left.wait_recv()
        nxt[...] = nbuf[...].astype(F32)

    @pl.when(p == 15)
    def _():
        nxt[...] = jnp.zeros_like(nxt)

    other = pl.multiple_of(HALF - c * HALF, 8)
    for step in range(1, OWNERS):
        source = (f + OWNERS - step) % OWNERS
        block = gath.at[source, pl.ds(other, HALF)]
        remote(block, block, csend.at[step], crecv.at[step], partner, f).wait_recv()
    for copy in out:
        copy.wait_send()

    @pl.when(p < 15)
    def _():
        right.wait_send()

    @pl.when(p > 0)
    def _():
        left.wait_send()


def spread(row):
    return jnp.broadcast_to(row, (8, LANES))


def sublane():
    return lax.broadcasted_iota(jnp.int32, (8, LANES), 0)


def tap_place(section, group, j):
    unit = section * 32 + group
    return unit // 6, pl.ds(64 + 6 * j + unit % 6, 1)


def own_rows(group, first, count):
    base = (group % 2) * MODES
    if count == MODES:
        base = pl.multiple_of(base, MODES)
    return group // 2, pl.ds(base + first, count)


def skip_place(group):
    return group // 2, pl.ds(82 + group % 2, 1)


def features(refs, cot_ref, gath, prev, xs, lanes, group):
    top = sublane() == 0
    raw, lag1, lag2, feat = [], [], [], []
    for q in range(3):
        xs[q, :, :] = refs[q][0, :, lanes].astype(F32)
        x = [xs[q, pl.ds(i, 8, stride=STEPS), :] for i in range(STEPS)]
        far = prev[pl.ds(q * 32 + group, 1), :]
        near = prev[pl.ds(96 + q * 32 + group, 1), :]
        before1 = jnp.where(top, spread(near), pltpu.roll(x[15], 1, 0))
        before2 = jnp.where(top, spread(far), pltpu.roll(x[14], 1, 0))
        one = [before1] + x[:15]
        two = [before2, before1] + x[:14]
        t = [spread(gath[tap_place(q, group, j)]) for j in range(3)]
        raw.append(x)
        lag1.append(one)
        lag2.append(two)
        feat.append([t[0] * x[i] + t[1] * one[i] + t[2] * two[i] for i in range(STEPS)])
    xs[3, :, :] = cot_ref[0, :, lanes].astype(F32)
    cot = [xs[3, pl.ds(i, 8, stride=STEPS), :] for i in range(STEPS)]
    return raw, lag1, lag2, feat, cot


def local_kernel(q_ref, k_ref, v_ref, cot_ref, gath, prev, ends, starts, e_out, s_out,
                 xs, us, gs, weights):
    block = pl.program_id(0)
    sub = sublane()

    def one(j, _):
        group = block * GROUPS + j
        lanes = pl.ds(pl.multiple_of(j * LANES, LANES), LANES)
        _, _, _, feat, cot = features((q_ref, k_ref, v_ref), cot_ref, gath, prev, xs, lanes, group)
        for i in range(STEPS):
            us[i] = feat[1][i] * feat[2][i]
            gs[i] = cot[i] * feat[0][i]
        rate = gath[own_rows(group, 32, MODES)]
        weights[0] = jnp.exp(-rate)
        weights[1] = jnp.exp(-16.0 * rate)
        weights[2] = jnp.exp(-32.0 * rate)
        weights[3] = jnp.exp(-64.0 * rate)
        for base in range(0, MODES, 8):
            modes = range(base, base + 8)
            d = [spread(weights[0, m : m + 1, :]) for m in modes]
            e = [us[0]] * 8
            b = [gs[15]] * 8
            for i in range(1, STEPS):
                u, g = us[i], gs[15 - i]
                e = [d[n] * e[n] + u for n in range(8)]
                b = [d[n] * b[n] + g for n in range(8)]
            for n, m in enumerate(modes):
                fwd, bwd = e[n], b[n]
                for power, shift in ((1, 1), (2, 2), (3, 4)):
                    w = spread(weights[power, m : m + 1, :])
                    fwd = fwd + jnp.where(sub >= shift, w, 0.0) * pltpu.roll(fwd, shift, 0)
                    bwd = bwd + jnp.where(sub < 8 - shift, w, 0.0) * pltpu.roll(bwd, 8 - shift, 0)
                ends[j, m] = fwd
                starts[j, m] = bwd
                e_out[own_rows(group, m, 1)] = fwd[7:8]
                s_out[own_rows(group, m, 1)] = bwd[0:1]
        return 0

    lax.fori_loop(0, GROUPS, one, 0)


def prefix_kernel(e_in, s_in, gath, before, after, e_prior, s_prior,
                  first, second, third, whole, last, agg, chip, begin, inner,
                  s1, r1, s2, r2, s3, r3, s4, r4, s5, r5):
    p, f, c, h, x = place()
    partner = p + 1 - 2 * c
    across = p + 2 - 4 * h
    n = jnp.where(c == 1, x, 3 - x)
    sign = jnp.where(c == 1, 4, -4)
    resident = h == c
    greet(partner, f)
    greet(across, f)
    for step in range(1, 4):
        greet((x + step) % 4 * 4 + 2 * h + c, f)
    pl.semaphore_wait(pltpu.get_barrier_semaphore(), 5)

    def piece(a):
        return pl.ds(a * PIECE, PIECE)

    def copy1(a, ref):
        return remote(ref.at[piece(a)], first.at[piece(a)], s1.at[a], r1.at[a], partner, f)

    def copy2(a):
        return remote(agg.at[piece(a)], second.at[piece(a)], s2.at[a], r2.at[a], across, f)

    def copy3(a, j):
        return remote(chip.at[piece(a)], third.at[j - 1, piece(a)], s3.at[j - 1, a], r3.at[j - 1, a],
                      p + sign * j, f)

    def copy4(a):
        return remote(begin.at[piece(a)], whole.at[piece(a)], s4.at[a], r4.at[a], across, f)

    def copy5(a, ref):
        return remote(ref.at[piece(a)], last.at[piece(a)], s5.at[a], r5.at[a], partner, f)

    def decay(a, power):
        return jnp.exp(gath[piece(a), 32:64, :] * (-128.0 * power))

    for a in range(PARTS):
        @pl.when(c == 0)
        def _():
            copy1(a, e_in).start()

        @pl.when(c == 1)
        def _():
            copy1(a, s_in).start()

    for a in range(PARTS):
        copy1(a, e_in).wait_recv()
        mine = jnp.where(c == 1, e_in[piece(a)], s_in[piece(a)])
        agg[piece(a)] = mine + decay(a, 1) * first[piece(a)]

        @pl.when(jnp.logical_not(resident))
        def _():
            copy2(a).start()

    for a in range(PARTS):
        @pl.when(resident)
        def _():
            copy2(a).wait_recv()
            chip[piece(a)] = agg[piece(a)] + decay(a, 2) * second[piece(a)]
            for j in range(1, 4):
                @pl.when(n + j < 4)
                def _():
                    copy3(a, j).start()

    for a in range(PARTS):
        @pl.when(resident)
        def _():
            for o in range(PIECE):
                for b in range(2):
                    at = (2 * (a * PIECE + o) + b) * LANES
                    cols = slice(at, at + LANES)
                    begin[a * PIECE + o, 16 * b : 16 * (b + 1), :] = jnp.where(
                        c == 1, before[0, :, cols], after[0, :, cols]
                    )
            span = decay(a, 4)
            for j in range(3, 0, -1):
                @pl.when(n >= j)
                def _():
                    copy3(a, j).wait_recv()
                    begin[piece(a)] = third[j - 1, piece(a)] + span * begin[piece(a)]
            copy4(a).start()
            inner[piece(a)] = decay(a, 2) * begin[piece(a)] + second[piece(a)]
            copy5(a, inner).start()

        @pl.when(jnp.logical_not(resident))
        def _():
            copy4(a).wait_recv()
            copy5(a, whole).start()

        head = jnp.where(resident, inner[piece(a)], whole[piece(a)])
        agg_own = decay(a, 1) * head + first[piece(a)]

        @pl.when(c == 1)
        def _():
            e_prior[piece(a)] = agg_own

        @pl.when(c == 0)
        def _():
            s_prior[piece(a)] = agg_own

    for a in range(PARTS):
        copy5(a, whole).wait_recv()

        @pl.when(c == 1)
        def _():
            s_prior[piece(a)] = last[piece(a)]

        @pl.when(c == 0)
        def _():
            e_prior[piece(a)] = last[piece(a)]

    for a in range(PARTS):
        copy1(a, e_in).wait_send()

        @pl.when(resident)
        def _():
            for j in range(1, 4):
                @pl.when(n + j < 4)
                def _():
                    copy3(a, j).wait_send()
            copy4(a).wait_send()

        @pl.when(jnp.logical_not(resident))
        def _():
            copy2(a).wait_send()
        copy5(a, whole).wait_send()


def row_sum(x):
    return jnp.sum(x, axis=0, keepdims=True)


def main_kernel(q_ref, k_ref, v_ref, cot_ref, gath, prev, nxt, ends, starts, e_in, e_prior, s_prior,
                out, grads, xs, us, gs, fs, hist, filt, back, weights):
    block = pl.program_id(0)
    sub = sublane()
    edge = lax.axis_index("ctx") == 15
    scale = 1.0 / math.sqrt(16 * 2048)

    def one(j, _):
        group = block * GROUPS + j
        lanes = pl.ds(pl.multiple_of(j * LANES, LANES), LANES)
        raw, lag1, lag2, feat, cot = features(
            (q_ref, k_ref, v_ref), cot_ref, gath, prev, xs, lanes, group
        )
        for i in range(STEPS):
            us[i] = feat[1][i] * feat[2][i]
            gs[i] = cot[i] * feat[0][i]
            fs[0, i] = feat[1][i]
            fs[1, i] = feat[2][i]
        whole = own_rows(group, 0, MODES)
        rate = gath[own_rows(group, 32, MODES)]
        res = gath[whole]
        decay = jnp.exp(-rate)
        weights[0] = decay
        blocks = sub.astype(F32) * -16.0
        blocks_back = (7 - sub).astype(F32) * -16.0
        for base in range(0, MODES, 8):
            modes = range(base, base + 8)
            d = [spread(weights[0, m : m + 1, :]) for m in modes]
            r = [spread(gath[own_rows(group, m, 1)]) for m in modes]
            state, leave = [], []
            for m in modes:
                speed = spread(gath[own_rows(group, 32 + m, 1)])
                inner = jnp.where(sub > 0, pltpu.roll(ends[j, m], 1, 0), 0.0)
                state.append(inner + jnp.exp(speed * blocks) * spread(e_prior[own_rows(group, m, 1)]))
                inner = jnp.where(sub < 7, pltpu.roll(starts[j, m], 7, 0), 0.0)
                leave.append(inner + jnp.exp(speed * blocks_back) * spread(s_prior[own_rows(group, m, 1)]))
            res_sum = [jnp.zeros((8, LANES), F32)] * 8
            rate_sum = [jnp.zeros((8, LANES), F32)] * 8
            for n in range(8):
                hist[n, 0] = state[n]
            for i in range(STEPS):
                u, g = us[i], gs[i]
                total = None
                for n in range(8):
                    state[n] = d[n] * state[n] + u
                    if i + 1 < STEPS:
                        hist[n, i + 1] = state[n]
                    res_sum[n] = res_sum[n] + g * state[n]
                    term = r[n] * state[n]
                    total = term if total is None else total + term
                filt[i] = total if base == 0 else filt[i] + total
            for i in range(STEPS - 1, -1, -1):
                g = gs[i]
                total = None
                for n in range(8):
                    leave[n] = d[n] * leave[n] + g
                    rate_sum[n] = rate_sum[n] + leave[n] * hist[n, i]
                    term = r[n] * leave[n]
                    total = term if total is None else total + term
                back[i] = total if base == 0 else back[i] + total
            for n, m in enumerate(modes):
                grads[own_rows(group, m, 1)] = row_sum(res_sum[n]) * scale
                grads[own_rows(group, 32 + m, 1)] = (
                    row_sum(rate_sum[n]) * (d[n][:1] * r[n][:1]) * -scale
                )
        skip_row = gath[skip_place(group)]
        skip = spread(skip_row)

        taps = [[gath[tap_place(q, group, t)] for t in range(3)] for q in range(3)]
        after = []
        for q in range(3):
            x = [xs[q, 126:127, :], xs[q, 127:128, :],
                 nxt[pl.ds(q * 32 + group, 1), :], nxt[pl.ds(96 + q * 32 + group, 1), :]]
            after.append([taps[q][0] * x[t] + taps[q][1] * x[t - 1] + taps[q][2] * x[t - 2] for t in (2, 3)])
        next_cot = [nxt[pl.ds(192 + t * 32 + group, 1), :] for t in range(2)]
        next_mixed = [after[1][t] * after[2][t] for t in range(2)]
        next_grad = [next_cot[t] * after[0][t] for t in range(2)]
        state0 = decay * (e_in[whole] + jnp.exp(rate * -128.0) * e_prior[whole]) + next_mixed[0]
        state1 = decay * state0 + next_mixed[1]
        back0 = s_prior[whole]
        back1 = (back0 - next_grad[0]) * jnp.exp(rate)
        follow = [[], [], []]
        for t, (s, b) in enumerate(((state0, back0), (state1, back1))):
            filtered = row_sum(res * s) + skip_row * next_mixed[t]
            mixed = row_sum(res * b) + skip_row * next_grad[t]
            follow[0].append(next_cot[t] * filtered)
            follow[1].append(mixed * after[2][t])
            follow[2].append(mixed * after[1][t])

        skip_sum = jnp.zeros((8, LANES), F32)
        grad = [[], [], []]
        for i in range(STEPS):
            u, g = us[i], gs[i]
            skip_sum = skip_sum + u * g
            mixed = back[i] + skip * g
            grad[0].append(xs[3, pl.ds(i, 8, stride=STEPS), :] * (filt[i] + skip * u))
            grad[1].append(mixed * fs[1, i])
            grad[2].append(mixed * fs[0, i])
        grads[skip_place(group)] = row_sum(skip_sum) * scale
        grads[group // 2, 84:96, :] = jnp.zeros((12, LANES), F32)
        for q in range(3):
            t = [spread(taps[q][k]) for k in range(3)]
            tail = []
            for k in range(2):
                row = jnp.where(edge, 0.0, follow[q][k])
                tail.append(jnp.where(sub == 7, spread(row), pltpu.roll(grad[q][k], 7, 0)))
            g = grad[q] + tail
            sums = [jnp.zeros((8, LANES), F32)] * 3
            for i in range(STEPS):
                sums[0] = sums[0] + raw[q][i] * g[i]
                sums[1] = sums[1] + lag1[q][i] * g[i]
                sums[2] = sums[2] + lag2[q][i] * g[i]
            for i in range(STEPS):
                xs[q, pl.ds(i, 8, stride=STEPS), :] = t[0] * g[i] + t[1] * g[i + 1] + t[2] * g[i + 2]
            for k in range(3):
                grads[tap_place(q, group, k)] = row_sum(sums[k]) * scale
            out[0, :, pl.ds(pl.multiple_of((q * 32 + group) * LANES, LANES), LANES)] = (
                xs[q].astype(jnp.bfloat16)
            )
        return 0

    lax.fori_loop(0, GROUPS, one, 0)


def reduce_kernel(part, out, chip, near, acc, shares, mine, sums, half,
                  s1, r1, s2, r2, s3, r3, s4, r4):
    p, f, c, _, _ = place()
    partner = p + 1 - 2 * c
    for step in range(1, OWNERS):
        greet(p, (f + step) % OWNERS)
    greet(partner, f)
    for step in range(1, 8):
        greet((p + 2 * step) % 16, f)
    pl.semaphore_wait(pltpu.get_barrier_semaphore(), 23)

    keep = pl.multiple_of(c * HALF, 8)
    give = pl.multiple_of(HALF - c * HALF, 8)
    pair = remote(part.at[:, pl.ds(give, HALF)], near, s1, r1, partner, f)
    pair.start()
    pair.wait_recv()
    out_copies = []
    acc[...] = part[:, pl.ds(keep, HALF), :] + near[...]
    for step in range(1, OWNERS):
        to = (f + step) % OWNERS
        copy = remote(acc.at[to], shares.at[f], s2.at[step], r2.at[step], p, to)
        copy.start()
        out_copies.append(copy)
    shares[f] = acc[f]
    for step in range(1, OWNERS):
        source = (f + OWNERS - step) % OWNERS
        remote(acc.at[f], shares.at[source], s2.at[step], r2.at[step], p, f).wait_recv()
    total = shares[0]
    for k in range(1, OWNERS):
        total = total + shares[k]
    me = p // 2
    sums[me] = total
    for step in range(1, 8):
        copy = remote(sums.at[me], sums.at[me], s3.at[step], r3.at[step], (p + 2 * step) % 16, f)
        copy.start()
        out_copies.append(copy)
    for step in range(1, 8):
        source = (me + 8 - step) % 8
        remote(sums.at[source], sums.at[source], s3.at[step], r3.at[step], p, f).wait_recv()
    total = sums[0]
    for k in range(1, 8):
        total = total + sums[k]
    out[pl.ds(keep, HALF), :] = total
    mine_ref = out.at[pl.ds(keep, HALF)]
    back = remote(mine_ref, mine_ref, s4, r4, partner, f)
    back.start()
    other = out.at[pl.ds(give, HALF)]
    remote(other, other, s4, r4, partner, f).wait_recv()
    back.wait_send()
    pair.wait_send()
    for copy in out_copies:
        copy.wait_send()


def shape(*dims, dtype=F32):
    return jax.ShapeDtypeStruct(dims, dtype)


def params(ident=None, limit=48):
    extra = {} if ident is None else {"collective_id": ident, "has_side_effects": True}
    return pltpu.CompilerParams(vmem_limit_bytes=limit * 2**20, **extra)


def per_device(rows_in, cotangent, taps, residues, rates, skip, state_before, adjoint_after):
    dma = pltpu.SemaphoreType.DMA
    bf16 = jnp.bfloat16
    tail = rows_in[0, 126:128].reshape(192, LANES)
    head = jnp.concatenate(
        [rows_in[0, 0:2].reshape(192, LANES), cotangent[0, 0:2].reshape(64, LANES)], axis=0
    )
    gath, prev, nxt = pl.pallas_call(
        gather_kernel,
        out_shape=(shape(OWNERS, ROWS, LANES), shape(192, LANES), shape(256, LANES)),
        in_specs=[VMEM] * 6,
        out_specs=(VMEM,) * 3,
        scratch_shapes=[
            pltpu.VMEM((192, LANES), bf16), pltpu.VMEM((256, LANES), bf16),
            dma((16,)), dma((16,)), dma((16,)), dma((16,)), dma((2,)), dma((2,)),
        ],
        compiler_params=params(1),
        name="gather",
    )(residues, rates, taps, skip[None, :], tail, head)

    width = GROUPS * LANES

    def section(q):
        return pl.BlockSpec((1, 128, width), lambda b, q=q: (0, 0, q * GRID + b))

    def fixed(*dims):
        return pl.BlockSpec(dims, lambda b: (0,) * len(dims))

    inner = pl.BlockSpec((GROUPS, MODES, 8, LANES), lambda b: (b, 0, 0, 0))
    small = (OWNERS, 2 * MODES, LANES)
    ends, starts, e_all, s_all = pl.pallas_call(
        local_kernel,
        grid=(GRID,),
        out_shape=(shape(32, MODES, 8, LANES), shape(32, MODES, 8, LANES), shape(*small), shape(*small)),
        in_specs=[section(0), section(1), section(2), section(0),
                  fixed(OWNERS, ROWS, LANES), fixed(192, LANES)],
        out_specs=(inner, inner, fixed(*small), fixed(*small)),
        scratch_shapes=[
            pltpu.VMEM((4, 128, LANES), F32), pltpu.VMEM((STEPS, 8, LANES), F32),
            pltpu.VMEM((STEPS, 8, LANES), F32), pltpu.VMEM((4, MODES, LANES), F32),
        ],
        compiler_params=params(),
        name="local",
    )(rows_in, rows_in, rows_in, cotangent, gath, prev)

    buf = pltpu.VMEM(small, F32)
    e_prior, s_prior = pl.pallas_call(
        prefix_kernel,
        out_shape=(shape(*small), shape(*small)),
        in_specs=[VMEM] * 5,
        out_specs=(VMEM,) * 2,
        scratch_shapes=[
            buf, buf, pltpu.VMEM((3,) + small, F32), buf, buf, buf, buf, buf, buf,
            dma((PARTS,)), dma((PARTS,)), dma((PARTS,)), dma((PARTS,)),
            dma((3, PARTS)), dma((3, PARTS)), dma((PARTS,)), dma((PARTS,)), dma((PARTS,)), dma((PARTS,)),
        ],
        compiler_params=params(2),
        name="prefix",
    )(e_all, s_all, gath, state_before, adjoint_after)

    vec = pltpu.VMEM((STEPS, 8, LANES), F32)
    grad_rows, grads = pl.pallas_call(
        main_kernel,
        grid=(GRID,),
        out_shape=(shape(1, 128, 12288, dtype=bf16), shape(OWNERS, ROWS, LANES)),
        in_specs=[section(0), section(1), section(2), section(0),
                  fixed(OWNERS, ROWS, LANES), fixed(192, LANES), fixed(256, LANES), inner, inner,
                  fixed(*small), fixed(*small), fixed(*small)],
        out_specs=(fixed(1, 128, 12288), fixed(OWNERS, ROWS, LANES)),
        scratch_shapes=[
            pltpu.VMEM((4, 128, LANES), F32), vec, vec, pltpu.VMEM((2, STEPS, 8, LANES), F32),
            pltpu.VMEM((8, STEPS, 8, LANES), F32), vec, vec, pltpu.VMEM((1, MODES, LANES), F32),
        ],
        compiler_params=params(),
        name="main",
    )(rows_in, rows_in, rows_in, cotangent, gath, prev, nxt, ends, starts, e_all, e_prior, s_prior)

    part = pltpu.VMEM((OWNERS, HALF, LANES), F32)
    total = pl.pallas_call(
        reduce_kernel,
        out_shape=shape(ROWS, LANES),
        in_specs=[VMEM],
        out_specs=VMEM,
        scratch_shapes=[
            part, part, part, part, part, pltpu.VMEM((8, HALF, LANES), F32), part,
            dma(()), dma(()), dma((16,)), dma((16,)), dma((8,)), dma((8,)), dma(()), dma(()),
        ],
        compiler_params=params(3),
        name="reduce",
    )(grads)
    return (
        grad_rows,
        total[64:82].reshape(3, 768),
        jnp.concatenate([total[0:16], total[16:32]], axis=1),
        jnp.concatenate([total[32:48], total[48:64]], axis=1),
        total[82:84].reshape(256),
    )


def solution(mesh):
    in_specs = (
        P("fsdp", "ctx", None),
        P("fsdp", "ctx", None),
        P(None, "fsdp"),
        P(None, "fsdp"),
        P(None, "fsdp"),
        P("fsdp"),
        P("fsdp", None, None),
        P("fsdp", None, None),
    )
    out_specs = (
        P("fsdp", "ctx", None),
        P(None, "fsdp"),
        P(None, "fsdp"),
        P(None, "fsdp"),
        P("fsdp"),
    )
    return jax.shard_map(
        per_device, mesh=mesh, in_specs=in_specs, out_specs=out_specs, check_vma=False
    )
```

```python
import math

import jax
import jax.numpy as jnp
from jax import lax
from jax.experimental import pallas as pl
from jax.experimental.pallas import tpu as pltpu
from jax.sharding import PartitionSpec as P

MESH = pl.DeviceIdType.MESH
F32 = jnp.float32
BF16 = jnp.bfloat16
MODES = 16
LANES = 128
STEPS = 16
OWNERS = 16
ROWS = 88
MODAL = 64
REST = ROWS - MODAL
WIDTH = 8
AHEAD = 4
STAGE1, STAGE2, STAGE3, STAGE4, STAGE5 = 1, 7, 10, 16, 17
MAIN = STAGE5 + 1
TURNS = MAIN + OWNERS
VMEM = pl.BlockSpec(memory_space=pltpu.VMEM)
ANY = pl.BlockSpec(memory_space=pl.ANY)


def remote(src, dst, send, recv, ctx, fsdp):
    return pltpu.make_async_remote_copy(
        src_ref=src, dst_ref=dst, send_sem=send, recv_sem=recv,
        device_id=(ctx, fsdp), device_id_type=MESH,
    )


def greet(ctx, fsdp):
    pl.semaphore_signal(
        pltpu.get_barrier_semaphore(), inc=1, device_id=(ctx, fsdp), device_id_type=MESH
    )


def spread(row):
    return jnp.broadcast_to(row, (8, LANES))


def spread_rows(rows):
    return jnp.broadcast_to(rows[:, None, :], (rows.shape[0], 8, LANES))


def sublane():
    return lax.broadcasted_iota(jnp.int32, (8, LANES), 0)


def row_sum(x):
    return jnp.sum(x, axis=0, keepdims=True)


def tree(terms):
    count = terms.shape[0]
    while count > 1:
        count //= 2
        terms = terms[:count] + terms[count:]
    return terms[0]


def tap_place(section, group, j):
    unit = section * 32 + group
    return unit // 6, pl.ds(MODAL + 6 * j + unit % 6, 1)


def own_rows(group, first, count):
    base = (group % 2) * MODES
    if count % 8 == 0:
        base = pl.multiple_of(base, MODES)
    return group // 2, pl.ds(base + first, count)


def lanes_of(unit, count=1):
    return pl.ds(pl.multiple_of(unit * LANES, LANES), count * LANES)


def local_pass(group, rows, cot, gath, prev, xs, X, F, U, G, C, ends, starts, e_all, s_all, weights):
    sub = sublane()
    top = sub == 0
    feat = []
    for q in range(3):
        unit = q * 32 + group
        xs[...] = rows[0, :, lanes_of(unit)].astype(F32)
        for i in range(STEPS):
            X[group, q, 2 + i] = xs[pl.ds(i, 8, stride=STEPS), :]
        near = spread(prev[pl.ds(96 + unit, 1), :])
        far = spread(prev[pl.ds(unit, 1), :])
        X[group, q, 1] = jnp.where(top, near, pltpu.roll(X[group, q, 17], 1, 0))
        X[group, q, 0] = jnp.where(top, far, pltpu.roll(X[group, q, 16], 1, 0))
        t = [spread(gath[tap_place(q, group, j)]) for j in range(3)]
        feat.append(t[0] * X[group, q, 2:18] + t[1] * X[group, q, 1:17] + t[2] * X[group, q, 0:16])
        if q:
            F[group, q - 1] = feat[q]
    xs[...] = cot[0, :, lanes_of(group)].astype(F32)
    for i in range(STEPS):
        C[group, i] = xs[pl.ds(i, 8, stride=STEPS), :]
    U[group] = feat[1] * feat[2]
    G[group] = C[group] * feat[0]
    rate = gath[own_rows(group, 32, MODES)]
    weights[0] = jnp.exp(-rate)
    weights[1] = jnp.exp(-16.0 * rate)
    weights[2] = jnp.exp(-32.0 * rate)
    weights[3] = jnp.exp(-64.0 * rate)
    d = spread_rows(weights[0])
    e = jnp.broadcast_to(U[group, 0], (MODES, 8, LANES))
    b = jnp.broadcast_to(G[group, 15], (MODES, 8, LANES))
    for i in range(1, STEPS):
        e = d * e + U[group, i]
        b = d * b + G[group, 15 - i]
    for power, shift in ((1, 1), (2, 2), (3, 4)):
        w = spread_rows(weights[power])
        e = e + jnp.where(sub >= shift, w, 0.0) * pltpu.roll(e, shift, 1)
        b = b + jnp.where(sub < 8 - shift, w, 0.0) * pltpu.roll(b, 8 - shift, 1)
    ends[group] = e
    starts[group] = b
    for n in range(MODES):
        e_all[own_rows(group, n, 1)] = e[n, 7:8]
        s_all[own_rows(group, n, 1)] = b[n, 0:1]


def main_pass(group, edge, gath, nxt, xs, X, F, U, G, C, ends, starts, e_all, e_prior, s_prior,
              out, grads, hist, filt, back, GB, weights):
    sub = sublane()
    scale = 1.0 / math.sqrt(16 * 2048)
    whole = own_rows(group, 0, MODES)
    rate = gath[own_rows(group, 32, MODES)]
    res = gath[whole]
    decay = jnp.exp(-rate)
    weights[0] = decay
    blocks = sub.astype(F32) * -16.0
    blocks_back = (7 - sub).astype(F32) * -16.0
    for base in range(0, MODES, WIDTH):
        some = slice(base, base + WIDTH)
        here = own_rows(group, base, WIDTH)
        d = spread_rows(weights[0, some])
        r = spread_rows(gath[here])
        speed = spread_rows(gath[own_rows(group, 32 + base, WIDTH)])
        state = jnp.where(sub > 0, pltpu.roll(ends[group, some], 1, 1), 0.0)
        state = state + jnp.exp(speed * blocks) * spread_rows(e_prior[here])
        leave = jnp.where(sub < 7, pltpu.roll(starts[group, some], 7, 1), 0.0)
        leave = leave + jnp.exp(speed * blocks_back) * spread_rows(s_prior[here])
        hist[0] = state
        res_sum = jnp.zeros((WIDTH, 8, LANES), F32)
        rate_sum = res_sum
        for i in range(STEPS):
            state = d * state + U[group, i]
            if i + 1 < STEPS:
                hist[i + 1] = state
            res_sum = res_sum + G[group, i] * state
            total = tree(r * state)
            filt[i] = total if base == 0 else filt[i] + total
        for i in range(STEPS - 1, -1, -1):
            leave = d * leave + G[group, i]
            rate_sum = rate_sum + leave * hist[i]
            total = tree(r * leave)
            back[i] = total if base == 0 else back[i] + total
        grads[here] = jnp.sum(res_sum, axis=1) * scale
        grads[own_rows(group, 32 + base, WIDTH)] = (
            jnp.sum(rate_sum, axis=1) * (weights[0, some] * gath[here]) * -scale
        )
    skip_at = (group // 2, pl.ds(82 + group % 2, 1))
    skip_row = gath[skip_at]
    skip = spread(skip_row)

    taps = [[gath[tap_place(q, group, t)] for t in range(3)] for q in range(3)]
    after = []
    for q in range(3):
        unit = q * 32 + group
        x = [X[group, q, 16, 7:8], X[group, q, 17, 7:8],
             nxt[pl.ds(unit, 1), :], nxt[pl.ds(96 + unit, 1), :]]
        after.append([taps[q][0] * x[t] + taps[q][1] * x[t - 1] + taps[q][2] * x[t - 2] for t in (2, 3)])
    next_cot = [nxt[pl.ds(192 + t * 32 + group, 1), :] for t in range(2)]
    next_mixed = [after[1][t] * after[2][t] for t in range(2)]
    next_grad = [next_cot[t] * after[0][t] for t in range(2)]
    state0 = decay * (e_all[whole] + jnp.exp(rate * -128.0) * e_prior[whole]) + next_mixed[0]
    state1 = decay * state0 + next_mixed[1]
    back0 = s_prior[whole]
    back1 = (back0 - next_grad[0]) * jnp.exp(rate)
    follow = [[], [], []]
    for t, (s, b) in enumerate(((state0, back0), (state1, back1))):
        filtered = row_sum(res * s) + skip_row * next_mixed[t]
        mixed = row_sum(res * b) + skip_row * next_grad[t]
        follow[0].append(next_cot[t] * filtered)
        follow[1].append(mixed * after[2][t])
        follow[2].append(mixed * after[1][t])

    u, g = U[group], G[group]
    grads[skip_at] = row_sum(jnp.sum(u * g, axis=0)) * scale
    mixed = back[...] + skip * g
    GB[0, 0:16] = C[group] * (filt[...] + skip * u)
    GB[1, 0:16] = mixed * F[group, 1]
    GB[2, 0:16] = mixed * F[group, 0]
    for q in range(3):
        t = [spread(taps[q][k]) for k in range(3)]
        for k in range(2):
            row = jnp.where(edge, 0.0, follow[q][k])
            GB[q, 16 + k] = jnp.where(sub == 7, spread(row), pltpu.roll(GB[q, k], 7, 0))
        grad = GB[q, 0:16]
        for k in range(3):
            terms = X[group, q, 2 - k : 18 - k] * grad
            grads[tap_place(q, group, k)] = row_sum(jnp.sum(terms, axis=0)) * scale
        y = t[0] * grad + t[1] * GB[q, 1:17] + t[2] * GB[q, 2:18]
        for i in range(STEPS):
            xs[pl.ds(i, 8, stride=STEPS), :] = y[i]
        out[0, :, lanes_of(q * 32 + group)] = xs[...].astype(BF16)


def kernel(rows_hbm, cot_hbm, taps, residues, rates, skip, before, after, rows_out, result,
           rows, cot, out, gath, grads, prev, nxt, tail_f, head_f, tail_b, head_b, prev_b, next_b,
           xs, X, F, U, G, C, ends, starts, e_all, s_all, e_prior, s_prior, hist, filt, back, GB, weights,
           first, second, third, whole, last, agg, chip, begin, inner,
           shares, shares_rest, sums, sums_rest, mine, other,
           in_sem, out_sem, halo_s, halo_r, rest_s, rest_r, modal_s, modal_r, hand_s, hand_r,
           s1, r1, s2, r2, s3, r3, s4, r4, s5, r5,
           share_s, share_r, share2_s, share2_r, sum_s, sum_r, sum2_s, sum2_r, end_s, end_r):
    p = lax.axis_index("ctx")
    f = lax.axis_index("fsdp")
    c, h, x = p % 2, (p // 2) % 2, p // 4
    partner = p + 1 - 2 * c
    across = p + 2 - 4 * h
    resident = h == c
    n = jnp.where(c == 1, x, 3 - x)
    sign = jnp.where(c == 1, 4, -4)
    edge = p == 15

    load_rows = pltpu.make_async_copy(rows_hbm, rows, in_sem.at[0])
    load_cot = pltpu.make_async_copy(cot_hbm, cot, in_sem.at[1])
    load_rows.start()
    load_cot.start()
    for step in range(1, OWNERS):
        greet(p, (f + step) % OWNERS)
    for step in range(1, 8):
        greet((p + 2 * step) % 16, f)
    greet(partner, f)
    greet((p + 15 + 2 * c) % 16, f)

    for b in range(2):
        cols = slice(LANES * b, LANES * (b + 1))
        gath[f, 16 * b : 16 * (b + 1), :] = residues[:, cols]
        gath[f, 32 + 16 * b : 48 + 16 * b, :] = rates[:, cols]
        gath[f, 82 + b : 83 + b, :] = skip[:, cols]
    for j in range(3):
        for b in range(6):
            row = MODAL + 6 * j + b
            gath[f, row : row + 1, :] = taps[j : j + 1, LANES * b : LANES * (b + 1)]
    gath[f, 84:88, :] = jnp.zeros((4, LANES), F32)
    for o in range(OWNERS):
        grads[o, 84:88, :] = jnp.zeros((4, LANES), F32)

    load_rows.wait()
    load_cot.wait()

    def edges(unit, _):
        end = rows[0, 112:128, lanes_of(unit)].astype(F32)
        tail_f[pl.ds(unit, 1), :] = end[14:15]
        tail_f[pl.ds(96 + unit, 1), :] = end[15:16]
        start = rows[0, 0:16, lanes_of(unit)].astype(F32)
        head_f[pl.ds(unit, 1), :] = start[0:1]
        head_f[pl.ds(96 + unit, 1), :] = start[1:2]
        return 0

    def edges_cot(unit, _):
        start = cot[0, 0:16, lanes_of(unit)].astype(F32)
        head_f[pl.ds(192 + unit, 1), :] = start[0:1]
        head_f[pl.ds(224 + unit, 1), :] = start[1:2]
        return 0

    lax.fori_loop(0, 96, edges, 0)
    lax.fori_loop(0, 32, edges_cot, 0)
    tail_b[...] = tail_f[...].astype(BF16)
    head_b[...] = head_f[...].astype(BF16)
    pl.semaphore_wait(pltpu.get_barrier_semaphore(), 24)

    right = remote(tail_b, prev_b, halo_s.at[0], halo_r.at[0], p + 1, f)
    left = remote(head_b, next_b, halo_s.at[1], halo_r.at[1], p - 1, f)

    @pl.when(p < 15)
    def _():
        right.start()

    @pl.when(p > 0)
    def _():
        left.start()

    def rest_copy(step, owner, to):
        block = gath.at[owner, pl.ds(MODAL, REST)]
        return remote(block, block, rest_s.at[step], rest_r.at[step], p, to)

    part = pl.multiple_of(32 - 32 * c, 32)
    part_other = pl.multiple_of(32 * c, 32)

    def modal_copy(step, owner, to):
        block = gath.at[owner, pl.ds(part, 32)]
        return remote(block, block, modal_s.at[step], modal_r.at[step], p, to)

    def hand_copy(step, rows_from):
        block = gath.at[(f + step) % OWNERS, pl.ds(rows_from, 32)]
        return remote(block, block, hand_s.at[step], hand_r.at[step], partner, f)

    for step in range(1, OWNERS):
        rest_copy(step, f, (f + OWNERS - step) % OWNERS).start()
    for step in range(1, OWNERS):
        modal_copy(step, f, (f + OWNERS - step) % OWNERS).start()

    @pl.when(p > 0)
    def _():
        right.wait_recv()
        prev[...] = prev_b[...].astype(F32)

    @pl.when(p == 0)
    def _():
        prev[...] = jnp.zeros_like(prev)

    @pl.when(p < 15)
    def _():
        left.wait_recv()
        nxt[...] = next_b[...].astype(F32)

    @pl.when(p == 15)
    def _():
        nxt[...] = jnp.zeros_like(nxt)

    for step in range(1, OWNERS):
        rest_copy(step, (f + step) % OWNERS, f).wait_recv()

    def hand_on(step):
        modal_copy(step, (f + step) % OWNERS, f).wait_recv()
        hand_copy(step, part).start()

    for step in range(1, 1 + AHEAD):
        hand_on(step)

    def copy1(o, ref):
        return remote(ref.at[o], first.at[o], s1.at[o], r1.at[o], partner, f)

    def copy2(o):
        return remote(agg.at[o], second.at[o], s2.at[o], r2.at[o], across, f)

    def copy3(o, j):
        return remote(chip.at[o], third.at[j - 1, o], s3.at[j - 1, o], r3.at[j - 1, o], p + sign * j, f)

    def copy4(o):
        return remote(begin.at[o], whole.at[o], s4.at[o], r4.at[o], across, f)

    def copy5(o, ref):
        return remote(ref.at[o], last.at[o], s5.at[o], r5.at[o], partner, f)

    def decay(o, power):
        return jnp.exp(gath[o, 32:64, :] * (-128.0 * power))

    def stage1(o):
        copy1(o, e_all).wait_recv()
        own = jnp.where(c == 1, e_all[o], s_all[o])
        agg[o] = own + decay(o, 1) * first[o]

        @pl.when(jnp.logical_not(resident))
        def _():
            copy2(o).start()

    def stage2(o):
        @pl.when(resident)
        def _():
            copy2(o).wait_recv()
            chip[o] = agg[o] + decay(o, 2) * second[o]
            for j in range(1, 4):
                @pl.when(n + j < 4)
                def _():
                    copy3(o, j).start()

    def own_prior(o, value):
        @pl.when(c == 1)
        def _():
            e_prior[o] = value

        @pl.when(c == 0)
        def _():
            s_prior[o] = value

    def stage3(o):
        @pl.when(resident)
        def _():
            for b in range(2):
                cols = lanes_of(2 * o + b)
                begin[o, 16 * b : 16 * (b + 1), :] = jnp.where(c == 1, before[0, :, cols], after[0, :, cols])
            span = decay(o, 4)
            for j in range(3, 0, -1):
                @pl.when(n >= j)
                def _():
                    copy3(o, j).wait_recv()
                    begin[o] = third[j - 1, o] + span * begin[o]
            copy4(o).start()
            inner[o] = decay(o, 2) * begin[o] + second[o]
            copy5(o, inner).start()
            own_prior(o, decay(o, 1) * inner[o] + first[o])

    def stage4(o):
        @pl.when(jnp.logical_not(resident))
        def _():
            copy4(o).wait_recv()
            copy5(o, whole).start()
            own_prior(o, decay(o, 1) * whole[o] + first[o])

    def stage5(o):
        copy5(o, whole).wait_recv()

        @pl.when(c == 1)
        def _():
            s_prior[o] = last[o]

        @pl.when(c == 0)
        def _():
            e_prior[o] = last[o]

    def share_copy(source, to):
        return remote(grads.at[to, pl.ds(0, MODAL)], shares.at[source],
                      share_s.at[to], share_r.at[source], p, to)

    def rest_share(source, to):
        return remote(grads.at[to, pl.ds(MODAL, REST)], shares_rest.at[source],
                      share2_s.at[to], share2_r.at[source], p, to)

    def out_copy(o, q):
        block = (slice(None), slice(None), lanes_of(q * 32 + 2 * o, 2))
        return pltpu.make_async_copy(out.at[block], rows_out.at[block], out_sem.at[q, o])

    def turn(t, _):
        @pl.when(t < OWNERS)
        def _():
            @pl.when(t + AHEAD + 1 < OWNERS)
            def _():
                hand_on(t + AHEAD + 1)

            @pl.when(t > 0)
            def _():
                hand_copy(t, part_other).wait_recv()
            o = (f + t) % OWNERS

            def one(j, _):
                local_pass(2 * o + j, rows, cot, gath, prev, xs, X, F, U, G, C, ends, starts,
                           e_all, s_all, weights)
                return 0

            lax.fori_loop(0, 2, one, 0)

            @pl.when(c == 0)
            def _():
                copy1(o, e_all).start()

            @pl.when(c == 1)
            def _():
                copy1(o, s_all).start()

        for stage, lag in ((stage5, STAGE5), (stage4, STAGE4), (stage3, STAGE3), (stage2, STAGE2),
                           (stage1, STAGE1)):
            @pl.when(jnp.logical_and(t >= lag, t < lag + OWNERS))
            def _():
                stage((f + t - lag) % OWNERS)

        @pl.when(t >= MAIN)
        def _():
            o = (f + t - MAIN + 1) % OWNERS

            def one(j, _):
                main_pass(2 * o + j, edge, gath, nxt, xs, X, F, U, G, C, ends, starts, e_all,
                          e_prior, s_prior, out, grads, hist, filt, back, GB, weights)
                return 0

            lax.fori_loop(0, 2, one, 0)
            for q in range(3):
                out_copy(o, q).start()

            @pl.when(t < TURNS - 1)
            def _():
                share_copy(f, o).start()

        return 0

    lax.fori_loop(0, TURNS, turn, 0)

    for step in range(1, OWNERS):
        rest_share(f, (f + step) % OWNERS).start()
    shares[f] = grads[f, 0:MODAL]
    shares_rest[f] = grads[f, MODAL:ROWS]
    for step in range(1, OWNERS):
        share_copy((f + step) % OWNERS, f).wait_recv()
    me = p // 2
    sums[me] = jnp.sum(shares[...], axis=0)

    def sum_copy(step, k, to):
        return remote(sums.at[k], sums.at[k], sum_s.at[step], sum_r.at[step], to, f)

    def sum_rest(step, k, to):
        return remote(sums_rest.at[k], sums_rest.at[k], sum2_s.at[step], sum2_r.at[step], to, f)

    for step in range(1, 8):
        sum_copy(step, me, (p + 2 * step) % 16).start()
    for step in range(1, OWNERS):
        rest_share((f + step) % OWNERS, f).wait_recv()
    sums_rest[me] = jnp.sum(shares_rest[...], axis=0)
    for step in range(1, 8):
        sum_rest(step, me, (p + 2 * step) % 16).start()
    for step in range(1, 8):
        sum_copy(step, (me + 8 - step) % 8, p).wait_recv()
    mine[0:MODAL] = jnp.sum(sums[...], axis=0)
    for step in range(1, 8):
        sum_rest(step, (me + 8 - step) % 8, p).wait_recv()
    mine[MODAL:ROWS] = jnp.sum(sums_rest[...], axis=0)
    end = remote(mine, other, end_s, end_r, partner, f)
    end.start()

    @pl.when(p < 15)
    def _():
        right.wait_send()

    @pl.when(p > 0)
    def _():
        left.wait_send()

    for step in range(1, OWNERS):
        to = (f + step) % OWNERS
        rest_copy(step, f, to).wait_send()
        modal_copy(step, f, to).wait_send()
        hand_copy(step, part).wait_send()
        share_copy(f, to).wait_send()
        rest_share(f, to).wait_send()

    def drain(o, _):
        copy1(o, e_all).wait_send()

        @pl.when(resident)
        def _():
            for j in range(1, 4):
                @pl.when(n + j < 4)
                def _():
                    copy3(o, j).wait_send()
            copy4(o).wait_send()

        @pl.when(jnp.logical_not(resident))
        def _():
            copy2(o).wait_send()
        copy5(o, whole).wait_send()
        for q in range(3):
            out_copy(o, q).wait()
        return 0

    lax.fori_loop(0, OWNERS, drain, 0)
    for step in range(1, 8):
        to = (p + 2 * step) % 16
        sum_copy(step, me, to).wait_send()
        sum_rest(step, me, to).wait_send()
    end.wait_recv()
    result[...] = mine[...] + other[...]
    end.wait_send()


def shape(*dims, dtype=F32):
    return jax.ShapeDtypeStruct(dims, dtype)


def per_device(rows_in, cotangent, taps, residues, rates, skip, state_before, adjoint_after):
    def buf(*dims, dtype=F32):
        return pltpu.VMEM(dims, dtype)

    def sems(*dims):
        return pltpu.SemaphoreType.DMA(dims)

    vec = buf(32, STEPS, 8, LANES)
    small = buf(OWNERS, 2 * MODES, LANES)
    each = [sems(16), sems(16)]
    grad_rows, total = pl.pallas_call(
        kernel,
        out_shape=(shape(1, 128, 12288, dtype=BF16), shape(ROWS, LANES)),
        in_specs=[ANY, ANY] + [VMEM] * 6,
        out_specs=(ANY, VMEM),
        scratch_shapes=[
            buf(1, 128, 12288, dtype=BF16), buf(1, 128, 4096, dtype=BF16), buf(1, 128, 12288, dtype=BF16),
            buf(OWNERS, ROWS, LANES), buf(OWNERS, ROWS, LANES), buf(192, LANES), buf(256, LANES),
            buf(192, LANES), buf(256, LANES), buf(192, LANES, dtype=BF16), buf(256, LANES, dtype=BF16),
            buf(192, LANES, dtype=BF16), buf(256, LANES, dtype=BF16),
            buf(128, LANES), buf(32, 3, 18, 8, LANES), buf(32, 2, STEPS, 8, LANES), vec, vec, vec,
            vec, vec, small, small, small, small, buf(STEPS, WIDTH, 8, LANES),
            buf(STEPS, 8, LANES), buf(STEPS, 8, LANES), buf(3, 18, 8, LANES), buf(4, MODES, LANES),
            small, small, buf(3, OWNERS, 2 * MODES, LANES), small, small, small, small, small, small,
            buf(OWNERS, MODAL, LANES), buf(OWNERS, REST, LANES), buf(8, MODAL, LANES), buf(8, REST, LANES),
            buf(ROWS, LANES), buf(ROWS, LANES),
            sems(2), sems(3, 16), sems(2), sems(2), *each, *each, *each,
            *each, *each, sems(3, 16), sems(3, 16), *each, *each,
            *each, *each, sems(8), sems(8), sems(8), sems(8), sems(), sems(),
        ],
        compiler_params=pltpu.CompilerParams(
            collective_id=1, has_side_effects=True, vmem_limit_bytes=56 * 2**20
        ),
        cost_estimate=pl.CostEstimate(flops=10**8, bytes_accessed=8 * 2**20, transcendentals=10**5),
        name="hyena",
    )(rows_in, cotangent, taps, residues, rates, skip[None, :], state_before, adjoint_after)
    return (
        grad_rows,
        total[64:82].reshape(3, 768),
        jnp.concatenate([total[0:16], total[16:32]], axis=1),
        jnp.concatenate([total[32:48], total[48:64]], axis=1),
        total[82:84].reshape(256),
    )


def solution(mesh):
    in_specs = (
        P("fsdp", "ctx", None),
        P("fsdp", "ctx", None),
        P(None, "fsdp"),
        P(None, "fsdp"),
        P(None, "fsdp"),
        P("fsdp"),
        P("fsdp", None, None),
        P("fsdp", None, None),
    )
    out_specs = (
        P("fsdp", "ctx", None),
        P(None, "fsdp"),
        P(None, "fsdp"),
        P(None, "fsdp"),
        P("fsdp"),
    )
    return jax.shard_map(
        per_device, mesh=mesh, in_specs=in_specs, out_specs=out_specs, check_vma=False
    )
```

```python
import math

import jax
import jax.numpy as jnp
from jax import lax
from jax.experimental import pallas as pl
from jax.experimental.pallas import tpu as pltpu
from jax.sharding import PartitionSpec as P

MESH = pl.DeviceIdType.MESH
F32 = jnp.float32
BF16 = jnp.bfloat16
MODES = 16
LANES = 128
STEPS = 16
OWNERS = 16
ROWS = 88
MODAL = 64
REST = ROWS - MODAL
WIDTH = 8
AHEAD = 4
STAGE1, STAGE2, STAGE3, STAGE4, STAGE5 = 1, 7, 10, 16, 17
MAIN = STAGE5 + 1
TURNS = MAIN + OWNERS
VMEM = pl.BlockSpec(memory_space=pltpu.VMEM)
ANY = pl.BlockSpec(memory_space=pl.ANY)


def remote(src, dst, send, recv, ctx, fsdp):
    return pltpu.make_async_remote_copy(
        src_ref=src, dst_ref=dst, send_sem=send, recv_sem=recv,
        device_id=(ctx, fsdp), device_id_type=MESH,
    )


def greet(ctx, fsdp):
    pl.semaphore_signal(
        pltpu.get_barrier_semaphore(), inc=1, device_id=(ctx, fsdp), device_id_type=MESH
    )


def spread(row):
    return jnp.broadcast_to(row, (8, LANES))


def spread_rows(rows):
    return jnp.broadcast_to(rows[:, None, :], (rows.shape[0], 8, LANES))


def sublane():
    return lax.broadcasted_iota(jnp.int32, (8, LANES), 0)


def row_sum(x):
    return jnp.sum(x, axis=0, keepdims=True)


def tree(terms):
    count = terms.shape[0]
    while count > 1:
        count //= 2
        terms = terms[:count] + terms[count:]
    return terms[0]


def tap_place(section, group, j):
    unit = section * 32 + group
    return unit // 6, pl.ds(MODAL + 6 * j + unit % 6, 1)


def own_rows(group, first, count):
    base = (group % 2) * MODES
    if count % 8 == 0:
        base = pl.multiple_of(base, MODES)
    return group // 2, pl.ds(base + first, count)


def lanes_of(unit, count=1):
    return pl.ds(pl.multiple_of(unit * LANES, LANES), count * LANES)


def local_pass(group, rows, cot, gath, prev, xs, X, F, U, G, C, ends, starts, e_all, s_all, weights):
    sub = sublane()
    top = sub == 0
    feat = []
    for q in range(3):
        unit = q * 32 + group
        xs[...] = rows[0, :, lanes_of(unit)].astype(F32)
        for i in range(STEPS):
            X[group, q, 2 + i] = xs[pl.ds(i, 8, stride=STEPS), :]
        near = spread(prev[pl.ds(96 + unit, 1), :])
        far = spread(prev[pl.ds(unit, 1), :])
        X[group, q, 1] = jnp.where(top, near, pltpu.roll(X[group, q, 17], 1, 0))
        X[group, q, 0] = jnp.where(top, far, pltpu.roll(X[group, q, 16], 1, 0))
        t = [spread(gath[tap_place(q, group, j)]) for j in range(3)]
        feat.append(t[0] * X[group, q, 2:18] + t[1] * X[group, q, 1:17] + t[2] * X[group, q, 0:16])
        if q:
            F[group, q - 1] = feat[q]
    xs[...] = cot[0, :, lanes_of(group)].astype(F32)
    for i in range(STEPS):
        C[group, i] = xs[pl.ds(i, 8, stride=STEPS), :]
    U[group] = feat[1] * feat[2]
    G[group] = C[group] * feat[0]
    rate = gath[own_rows(group, 32, MODES)]
    weights[0] = jnp.exp(-rate)
    weights[1] = jnp.exp(-16.0 * rate)
    weights[2] = jnp.exp(-32.0 * rate)
    weights[3] = jnp.exp(-64.0 * rate)
    d = spread_rows(weights[0])
    e = jnp.broadcast_to(U[group, 0], (MODES, 8, LANES))
    b = jnp.broadcast_to(G[group, 15], (MODES, 8, LANES))
    for i in range(1, STEPS):
        e = d * e + U[group, i]
        b = d * b + G[group, 15 - i]
    for power, shift in ((1, 1), (2, 2), (3, 4)):
        w = spread_rows(weights[power])
        e = e + jnp.where(sub >= shift, w, 0.0) * pltpu.roll(e, shift, 1)
        b = b + jnp.where(sub < 8 - shift, w, 0.0) * pltpu.roll(b, 8 - shift, 1)
    ends[group] = e
    starts[group] = b
    for n in range(MODES):
        e_all[own_rows(group, n, 1)] = e[n, 7:8]
        s_all[own_rows(group, n, 1)] = b[n, 0:1]


def main_pass(group, edge, gath, nxt, xs, X, F, U, G, C, ends, starts, e_all, e_prior, s_prior,
              grads, hist, filt, back, GB, weights):
    sub = sublane()
    scale = 1.0 / math.sqrt(16 * 2048)
    whole = own_rows(group, 0, MODES)
    rate = gath[own_rows(group, 32, MODES)]
    res = gath[whole]
    decay = jnp.exp(-rate)
    weights[0] = decay
    blocks = sub.astype(F32) * -16.0
    blocks_back = (7 - sub).astype(F32) * -16.0
    for base in range(0, MODES, WIDTH):
        some = slice(base, base + WIDTH)
        here = own_rows(group, base, WIDTH)
        d = spread_rows(weights[0, some])
        r = spread_rows(gath[here])
        speed = spread_rows(gath[own_rows(group, 32 + base, WIDTH)])
        state = jnp.where(sub > 0, pltpu.roll(ends[group, some], 1, 1), 0.0)
        state = state + jnp.exp(speed * blocks) * spread_rows(e_prior[here])
        leave = jnp.where(sub < 7, pltpu.roll(starts[group, some], 7, 1), 0.0)
        leave = leave + jnp.exp(speed * blocks_back) * spread_rows(s_prior[here])
        hist[0] = state
        res_sum = jnp.zeros((WIDTH, 8, LANES), F32)
        rate_sum = res_sum
        for i in range(STEPS):
            state = d * state + U[group, i]
            if i + 1 < STEPS:
                hist[i + 1] = state
            res_sum = res_sum + G[group, i] * state
            total = tree(r * state)
            filt[i] = total if base == 0 else filt[i] + total
        for i in range(STEPS - 1, -1, -1):
            leave = d * leave + G[group, i]
            rate_sum = rate_sum + leave * hist[i]
            total = tree(r * leave)
            back[i] = total if base == 0 else back[i] + total
        grads[here] = jnp.sum(res_sum, axis=1) * scale
        grads[own_rows(group, 32 + base, WIDTH)] = (
            jnp.sum(rate_sum, axis=1) * (weights[0, some] * gath[here]) * -scale
        )
    skip_at = (group // 2, pl.ds(82 + group % 2, 1))
    skip_row = gath[skip_at]
    skip = spread(skip_row)

    taps = [[gath[tap_place(q, group, t)] for t in range(3)] for q in range(3)]
    after = []
    for q in range(3):
        unit = q * 32 + group
        x = [X[group, q, 16, 7:8], X[group, q, 17, 7:8],
             nxt[pl.ds(unit, 1), :], nxt[pl.ds(96 + unit, 1), :]]
        after.append([taps[q][0] * x[t] + taps[q][1] * x[t - 1] + taps[q][2] * x[t - 2] for t in (2, 3)])
    next_cot = [nxt[pl.ds(192 + t * 32 + group, 1), :] for t in range(2)]
    next_mixed = [after[1][t] * after[2][t] for t in range(2)]
    next_grad = [next_cot[t] * after[0][t] for t in range(2)]
    state0 = decay * (e_all[whole] + jnp.exp(rate * -128.0) * e_prior[whole]) + next_mixed[0]
    state1 = decay * state0 + next_mixed[1]
    back0 = s_prior[whole]
    back1 = (back0 - next_grad[0]) * jnp.exp(rate)
    follow = [[], [], []]
    for t, (s, b) in enumerate(((state0, back0), (state1, back1))):
        filtered = row_sum(res * s) + skip_row * next_mixed[t]
        mixed = row_sum(res * b) + skip_row * next_grad[t]
        follow[0].append(next_cot[t] * filtered)
        follow[1].append(mixed * after[2][t])
        follow[2].append(mixed * after[1][t])

    u, g = U[group], G[group]
    grads[skip_at] = row_sum(jnp.sum(u * g, axis=0)) * scale
    mixed = back[...] + skip * g
    GB[group, 0, 0:16] = C[group] * (filt[...] + skip * u)
    GB[group, 1, 0:16] = mixed * F[group, 1]
    GB[group, 2, 0:16] = mixed * F[group, 0]
    for q in range(3):
        for k in range(2):
            row = jnp.where(edge, 0.0, follow[q][k])
            GB[group, q, 16 + k] = jnp.where(sub == 7, spread(row), pltpu.roll(GB[group, q, k], 7, 0))
        grad = GB[group, q, 0:16]
        for k in range(3):
            terms = X[group, q, 2 - k : 18 - k] * grad
            grads[tap_place(q, group, k)] = row_sum(jnp.sum(terms, axis=0)) * scale


def rows_pass(group, gath, xs, GB, out):
    for q in range(3):
        t = [spread(gath[tap_place(q, group, k)]) for k in range(3)]
        y = t[0] * GB[group, q, 0:16] + t[1] * GB[group, q, 1:17] + t[2] * GB[group, q, 2:18]
        for i in range(STEPS):
            xs[pl.ds(i, 8, stride=STEPS), :] = y[i]
        out[0, :, lanes_of(q * 32 + group)] = xs[...].astype(BF16)


def kernel(rows_hbm, cot_hbm, taps, residues, rates, skip, before_hbm, after_hbm,
           rows_out, result,
           rows, cot, before, after, out, gath, grads, prev, nxt, tail_f, head_f, tail_b, head_b, prev_b, next_b,
           xs, X, F, U, G, C, ends, starts, e_all, s_all, e_prior, s_prior, hist, filt, back, GB, weights,
           first, second, third, whole, last, agg, chip, begin, inner, span,
           by_y, by_z, relay, rest_y, rest_z, rest_sum, modal_x, modal_across, rest_x, rest_across,
           mine, other,
           in_sem, out_sem, halo_s, halo_r, rest_s, rest_r, modal_s, modal_r, hand_s, hand_r,
           s1, r1, s2, r2, s3, r3, s4, r4, s5, r5,
           ys, yr, zs, zr, rys, ryr, rzs, rzr, mxs, mxr, mas, mar, rxs, rxr, ras, rar, end_s, end_r):
    p = lax.axis_index("ctx")
    f = lax.axis_index("fsdp")
    c, h, x = p % 2, (p // 2) % 2, p // 4
    partner = p + 1 - 2 * c
    across = p + 2 - 4 * h
    resident = h == c
    n = jnp.where(c == 1, x, 3 - x)
    sign = jnp.where(c == 1, 4, -4)
    edge = p == 15
    y, z = f // 4, f % 4
    z_peers = [y * 4 + (z + k) % 4 for k in range(1, 4)]
    y_peers = [(y + k) % 4 * 4 + z for k in range(1, 4)]

    def owner_at(k):
        turn_z = (k // 4 + 1) % 4
        turn_y = (k + k // 12) % 4
        return (y + turn_y) % 4 * 4 + (z + turn_z) % 4

    def local_at(k):
        return owner_at((k + 15) % 16)

    load_rows = pltpu.make_async_copy(rows_hbm, rows, in_sem.at[0])
    load_cot = pltpu.make_async_copy(cot_hbm, cot, in_sem.at[1])
    load_before = pltpu.make_async_copy(before_hbm, before, in_sem.at[2])
    load_after = pltpu.make_async_copy(after_hbm, after, in_sem.at[3])
    for load in (load_rows, load_cot, load_before, load_after):
        load.start()
    for peer in z_peers + y_peers:
        greet(p, peer)
    for step in range(1, 4):
        greet((p + 4 * step) % 16, f)
    greet(across, f)
    greet(partner, f)
    greet((p + 15 + 2 * c) % 16, f)

    for b in range(2):
        cols = slice(LANES * b, LANES * (b + 1))
        gath[f, 16 * b : 16 * (b + 1), :] = residues[:, cols]
        gath[f, 32 + 16 * b : 48 + 16 * b, :] = rates[:, cols]
        gath[f, 82 + b : 83 + b, :] = skip[:, cols]
    for j in range(3):
        for b in range(6):
            row = MODAL + 6 * j + b
            gath[f, row : row + 1, :] = taps[j : j + 1, LANES * b : LANES * (b + 1)]
    gath[f, 84:88, :] = jnp.zeros((4, LANES), F32)
    for o in range(OWNERS):
        grads[o, 84:88, :] = jnp.zeros((4, LANES), F32)

    pl.semaphore_wait(pltpu.get_barrier_semaphore(), 12)

    def rest_copy(k, owner, to):
        block = gath.at[owner, pl.ds(MODAL, REST)]
        return remote(block, block, rest_s.at[k], rest_r.at[owner], p, to)

    part = pl.multiple_of(32 - 32 * c, 32)
    part_other = pl.multiple_of(32 * c, 32)

    def modal_copy(k, owner, to):
        block = gath.at[owner, pl.ds(part, 32)]
        return remote(block, block, modal_s.at[k], modal_r.at[owner], p, to)

    def hand_copy(owner, rows_from):
        block = gath.at[owner, pl.ds(rows_from, 32)]
        return remote(block, block, hand_s.at[owner], hand_r.at[owner], partner, f)

    for make in (rest_copy, modal_copy):
        for k, peer in enumerate(z_peers + y_peers):
            make(k, f, peer).start()

    for load in (load_rows, load_cot, load_before, load_after):
        load.wait()

    def edges(unit, _):
        end = rows[0, 112:128, lanes_of(unit)].astype(F32)
        tail_f[pl.ds(unit, 1), :] = end[14:15]
        tail_f[pl.ds(96 + unit, 1), :] = end[15:16]
        start = rows[0, 0:16, lanes_of(unit)].astype(F32)
        head_f[pl.ds(unit, 1), :] = start[0:1]
        head_f[pl.ds(96 + unit, 1), :] = start[1:2]
        return 0

    def edges_cot(unit, _):
        start = cot[0, 0:16, lanes_of(unit)].astype(F32)
        head_f[pl.ds(192 + unit, 1), :] = start[0:1]
        head_f[pl.ds(224 + unit, 1), :] = start[1:2]
        return 0

    lax.fori_loop(0, 96, edges, 0, unroll=4)
    lax.fori_loop(0, 32, edges_cot, 0, unroll=4)
    tail_b[...] = tail_f[...].astype(BF16)
    head_b[...] = head_f[...].astype(BF16)

    right = remote(tail_b, prev_b, halo_s.at[0], halo_r.at[0], p + 1, f)
    left = remote(head_b, next_b, halo_s.at[1], halo_r.at[1], p - 1, f)

    @pl.when(p < 15)
    def _():
        right.start()

    @pl.when(p > 0)
    def _():
        left.start()

    for make in (rest_copy, modal_copy):
        for k, owner in enumerate(z_peers):
            make(0, owner, f).wait_recv()
            for j, peer in enumerate(y_peers):
                make(6 + 3 * k + j, owner, peer).start()

    @pl.when(p > 0)
    def _():
        right.wait_recv()
        prev[...] = prev_b[...].astype(F32)

    @pl.when(p == 0)
    def _():
        prev[...] = jnp.zeros_like(prev)

    @pl.when(p < 15)
    def _():
        left.wait_recv()
        nxt[...] = next_b[...].astype(F32)

    @pl.when(p == 15)
    def _():
        nxt[...] = jnp.zeros_like(nxt)

    for k in range(4):
        for peer in y_peers:
            rest_copy(0, peer // 4 * 4 + (z + k) % 4, f).wait_recv()

    def hand_on(owner):
        @pl.when(owner // 4 != y)
        def _():
            modal_copy(0, owner, f).wait_recv()
        hand_copy(owner, part).start()

    for k in range(1, 1 + AHEAD):
        hand_on(local_at(k))

    def copy1(o, ref):
        return remote(ref.at[o], first.at[o], s1.at[o], r1.at[o], partner, f)

    def copy2(o):
        return remote(agg.at[o], second.at[o], s2.at[o], r2.at[o], across, f)

    def copy3(o, j):
        return remote(chip.at[o], third.at[j - 1, o], s3.at[j - 1, o], r3.at[j - 1, o], p + sign * j, f)

    def copy4(o):
        return remote(begin.at[o], whole.at[o], s4.at[o], r4.at[o], across, f)

    def copy5(o, ref):
        return remote(ref.at[o], last.at[o], s5.at[o], r5.at[o], partner, f)

    def decay(o, power):
        value = span[o]
        for _ in range(power // 2):
            value = value * value
        return value

    def stage1(o):
        copy1(o, e_all).wait_recv()
        span[o] = jnp.exp(gath[o, 32:64, :] * -128.0)
        own = jnp.where(c == 1, e_all[o], s_all[o])
        agg[o] = own + decay(o, 1) * first[o]

        @pl.when(jnp.logical_not(resident))
        def _():
            copy2(o).start()

    def stage2(o):
        @pl.when(resident)
        def _():
            copy2(o).wait_recv()
            chip[o] = agg[o] + decay(o, 2) * second[o]
            for j in range(1, 4):
                @pl.when(n + j < 4)
                def _():
                    copy3(o, j).start()

    def own_prior(o, value):
        @pl.when(c == 1)
        def _():
            e_prior[o] = value

        @pl.when(c == 0)
        def _():
            s_prior[o] = value

    def stage3(o):
        @pl.when(resident)
        def _():
            for b in range(2):
                cols = lanes_of(2 * o + b)
                begin[o, 16 * b : 16 * (b + 1), :] = jnp.where(c == 1, before[0, :, cols], after[0, :, cols])
            four = decay(o, 4)
            for j in range(3, 0, -1):
                @pl.when(n >= j)
                def _():
                    copy3(o, j).wait_recv()
                    begin[o] = third[j - 1, o] + four * begin[o]
            copy4(o).start()
            inner[o] = decay(o, 2) * begin[o] + second[o]
            copy5(o, inner).start()
            own_prior(o, decay(o, 1) * inner[o] + first[o])

    def stage4(o):
        @pl.when(jnp.logical_not(resident))
        def _():
            copy4(o).wait_recv()
            copy5(o, whole).start()
            own_prior(o, decay(o, 1) * whole[o] + first[o])

    def stage5(o):
        copy5(o, whole).wait_recv()

        @pl.when(c == 1)
        def _():
            s_prior[o] = last[o]

        @pl.when(c == 0)
        def _():
            e_prior[o] = last[o]

    def share_copy(owner, source, to):
        return remote(grads.at[owner, pl.ds(0, MODAL)], by_y.at[owner % 4, source],
                      ys.at[owner], yr.at[owner % 4, source], p, to)

    def relay_copy(to_z, from_z):
        return remote(relay.at[to_z], by_z.at[from_z], zs.at[to_z], zr.at[from_z], p, y * 4 + to_z)

    def gather_y(owner):
        for k in range(1, 4):
            share_copy(owner, (y + k) % 4, f).wait_recv()
        by_y[owner % 4, y] = grads[owner, 0:MODAL]
        return jnp.sum(by_y[owner % 4], axis=0)

    def relay_one(to_z):
        relay[to_z] = gather_y(y * 4 + to_z)
        relay_copy(to_z, z).start()

    def write_rows(begin_group, end_group):
        def one(group, _):
            rows_pass(group, gath, xs, GB, out)
            return 0

        lax.fori_loop(begin_group, end_group, one, 0)

    def turn(t, _):
        @pl.when(t < OWNERS)
        def _():
            @pl.when(t + AHEAD + 1 < OWNERS)
            def _():
                hand_on(local_at(t + AHEAD + 1))
            o = local_at(t)

            @pl.when(t > 0)
            def _():
                hand_copy(o, part_other).wait_recv()

            def one(j, _):
                local_pass(2 * o + j, rows, cot, gath, prev, xs, X, F, U, G, C, ends, starts,
                           e_all, s_all, weights)
                return 0

            lax.fori_loop(0, 2, one, 0)

            @pl.when(c == 0)
            def _():
                copy1(o, e_all).start()

            @pl.when(c == 1)
            def _():
                copy1(o, s_all).start()

        for stage, lag in ((stage5, STAGE5), (stage4, STAGE4), (stage3, STAGE3), (stage2, STAGE2),
                           (stage1, STAGE1)):
            @pl.when(jnp.logical_and(t >= lag, t < lag + OWNERS))
            def _():
                stage(local_at(t - lag))

        @pl.when(t >= MAIN)
        def _():
            o = owner_at(t - MAIN)

            def one(j, _):
                main_pass(2 * o + j, edge, gath, nxt, xs, X, F, U, G, C, ends, starts, e_all,
                          e_prior, s_prior, grads, hist, filt, back, GB, weights)
                return 0

            lax.fori_loop(0, 2, one, 0)

            @pl.when(o // 4 != y)
            def _():
                share_copy(o, y, o // 4 * 4 + z).start()

        for k in range(1, 4):
            @pl.when(t == MAIN + 4 * k + 1)
            def _():
                relay_one((z + k) % 4)

        return 0

    lax.fori_loop(0, TURNS, turn, 0)

    def rest_to_y(to_y, from_y):
        return remote(grads.at[pl.ds(4 * to_y, 4), pl.ds(MODAL, REST)], rest_y.at[from_y],
                      rys.at[to_y], ryr.at[from_y], p, to_y * 4 + z)

    def rest_to_z(to_z, from_z):
        return remote(rest_sum.at[to_z], rest_z.at[from_z], rzs.at[to_z], rzr.at[from_z], p, y * 4 + to_z)

    def over_x(ref, send, recv, k, slot):
        return remote(ref.at[slot], ref.at[slot], send.at[k], recv.at[slot], (p + 4 * k) % 16, f)

    def over_across(ref, send, recv, slot):
        return remote(ref.at[slot], ref.at[slot], send, recv, across, f)

    for k in range(1, 4):
        rest_to_y((y + k) % 4, y).start()
    write_rows(0, 10)
    total = gather_y(f)
    for k in range(1, 4):
        relay_copy(z, (z + k) % 4).wait_recv()
    by_z[z] = total
    modal_x[x] = jnp.sum(by_z[...], axis=0)
    for k in range(1, 4):
        over_x(modal_x, mxs, mxr, k, x).start()

    rest_y[y] = grads[pl.ds(4 * y, 4), MODAL:ROWS, :]
    for k in range(1, 4):
        rest_to_y(y, (y + k) % 4).wait_recv()
    rest_sum[...] = jnp.sum(rest_y[...], axis=0)
    for k in range(1, 4):
        rest_to_z((z + k) % 4, z).start()
    write_rows(10, 22)

    for k in range(1, 4):
        over_x(modal_x, mxs, mxr, k, (x + k) % 4).wait_recv()
    modal_across[h] = jnp.sum(modal_x[...], axis=0)
    over_across(modal_across, mas, mar, h).start()

    rest_z[z] = rest_sum[z]
    for k in range(1, 4):
        rest_to_z(z, (z + k) % 4).wait_recv()
    rest_x[x] = jnp.sum(rest_z[...], axis=0)
    for k in range(1, 4):
        over_x(rest_x, rxs, rxr, k, x).start()
    write_rows(22, 32)
    store = pltpu.make_async_copy(out, rows_out, out_sem)
    store.start()

    over_across(modal_across, mas, mar, 1 - h).wait_recv()
    mine[0:MODAL] = modal_across[0] + modal_across[1]

    for k in range(1, 4):
        over_x(rest_x, rxs, rxr, k, (x + k) % 4).wait_recv()
    rest_across[h] = jnp.sum(rest_x[...], axis=0)
    over_across(rest_across, ras, rar, h).start()
    over_across(rest_across, ras, rar, 1 - h).wait_recv()
    mine[MODAL:ROWS] = rest_across[0] + rest_across[1]
    end = remote(mine, other, end_s, end_r, partner, f)
    end.start()

    @pl.when(p < 15)
    def _():
        right.wait_send()

    @pl.when(p > 0)
    def _():
        left.wait_send()

    for k in range(15):
        rest_copy(k, f, f).wait_send()
        modal_copy(k, f, f).wait_send()
    for k in range(1, 4):
        relay_copy((z + k) % 4, z).wait_send()
        rest_to_y((y + k) % 4, y).wait_send()
        rest_to_z((z + k) % 4, z).wait_send()
        over_x(modal_x, mxs, mxr, k, x).wait_send()
        over_x(rest_x, rxs, rxr, k, x).wait_send()
    over_across(modal_across, mas, mar, h).wait_send()
    over_across(rest_across, ras, rar, h).wait_send()

    def drain(o, _):
        copy1(o, e_all).wait_send()

        @pl.when(resident)
        def _():
            for j in range(1, 4):
                @pl.when(n + j < 4)
                def _():
                    copy3(o, j).wait_send()
            copy4(o).wait_send()

        @pl.when(jnp.logical_not(resident))
        def _():
            copy2(o).wait_send()
        copy5(o, whole).wait_send()

        @pl.when(o != f)
        def _():
            hand_copy(o, part).wait_send()

        @pl.when(o // 4 != y)
        def _():
            share_copy(o, y, f).wait_send()
        return 0

    lax.fori_loop(0, OWNERS, drain, 0)
    store.wait()
    end.wait_recv()
    result[...] = mine[...] + other[...]
    end.wait_send()


def finish(rows_in, mine, rows_out, taps_out, res_out, rate_out, skip_out, held, load_sem, store_sem):
    def piece(k):
        return slice(None), slice(16 * k, 16 * (k + 1))

    loads = [pltpu.make_async_copy(rows_in.at[piece(k)], held.at[piece(k)], load_sem.at[k]) for k in range(8)]
    stores = [pltpu.make_async_copy(held.at[piece(k)], rows_out.at[piece(k)], store_sem.at[k]) for k in range(8)]
    for load in loads:
        load.start()
    for b in range(2):
        cols = slice(LANES * b, LANES * (b + 1))
        res_out[:, cols] = mine[16 * b : 16 * (b + 1), :]
        rate_out[:, cols] = mine[32 + 16 * b : 48 + 16 * b, :]
        skip_out[:, cols] = mine[82 + b : 83 + b, :]
    for j in range(3):
        for b in range(6):
            row = MODAL + 6 * j + b
            taps_out[j : j + 1, LANES * b : LANES * (b + 1)] = mine[row : row + 1, :]
    for load, store in zip(loads, stores):
        load.wait()
        store.start()
    for store in stores:
        store.wait()

def shape(*dims, dtype=F32):
    return jax.ShapeDtypeStruct(dims, dtype)


def per_device(rows_in, cotangent, taps, residues, rates, skip, state_before, adjoint_after):
    def buf(*dims, dtype=F32):
        return pltpu.VMEM(dims, dtype)

    def sems(*dims):
        return pltpu.SemaphoreType.DMA(dims)

    vec = buf(32, STEPS, 8, LANES)
    small = buf(OWNERS, 2 * MODES, LANES)
    each = [sems(16), sems(16)]
    four = [sems(4), sems(4)]
    one = [sems(), sems()]
    rows_sum, total = pl.pallas_call(
        kernel,
        out_shape=(shape(1, 128, 12288, dtype=BF16), shape(ROWS, LANES)),
        in_specs=[ANY, ANY] + [VMEM] * 4 + [ANY, ANY],
        out_specs=(ANY, VMEM),
        scratch_shapes=[
            buf(1, 128, 12288, dtype=BF16), buf(1, 128, 4096, dtype=BF16), buf(1, MODES, 4096), buf(1, MODES, 4096),
            buf(1, 128, 12288, dtype=BF16),
            buf(OWNERS, ROWS, LANES), buf(OWNERS, ROWS, LANES), buf(192, LANES), buf(256, LANES),
            buf(192, LANES), buf(256, LANES), buf(192, LANES, dtype=BF16), buf(256, LANES, dtype=BF16),
            buf(192, LANES, dtype=BF16), buf(256, LANES, dtype=BF16),
            buf(128, LANES), buf(32, 3, 18, 8, LANES), buf(32, 2, STEPS, 8, LANES), vec, vec, vec,
            vec, vec, small, small, small, small, buf(STEPS, WIDTH, 8, LANES),
            buf(STEPS, 8, LANES), buf(STEPS, 8, LANES), buf(32, 3, 18, 8, LANES), buf(4, MODES, LANES),
            small, small, buf(3, OWNERS, 2 * MODES, LANES), small, small, small, small, small, small, small,
            buf(4, 4, MODAL, LANES), buf(4, MODAL, LANES), buf(4, MODAL, LANES),
            buf(4, 4, REST, LANES), buf(4, REST, LANES), buf(4, REST, LANES),
            buf(4, MODAL, LANES), buf(2, MODAL, LANES), buf(4, REST, LANES), buf(2, REST, LANES),
            buf(ROWS, LANES), buf(ROWS, LANES),
            sems(4), sems(), sems(2), sems(2), *each, *each, *each,
            *each, *each, sems(3, 16), sems(3, 16), *each, *each,
            sems(16), sems(4, 4), *four, *four, *four, *four, *one, *four, *one, *one,
        ],
        compiler_params=pltpu.CompilerParams(
            collective_id=1, has_side_effects=True, vmem_limit_bytes=56 * 2**20
        ),
        cost_estimate=pl.CostEstimate(flops=10**8, bytes_accessed=8 * 2**20, transcendentals=10**5),
        name="hyena",
    )(rows_in, cotangent, taps, residues, rates, skip[None, :], state_before, adjoint_after)
    grad_rows, taps_sum, res_sum, rate_sum, skip_sum = pl.pallas_call(
        finish,
        out_shape=(shape(1, 128, 12288, dtype=BF16), shape(3, 768), shape(16, 256), shape(16, 256),
                   shape(1, 256)),
        in_specs=[ANY, VMEM],
        out_specs=(ANY,) + (VMEM,) * 4,
        scratch_shapes=[buf(1, 128, 12288, dtype=BF16), sems(8), sems(8)],
        compiler_params=pltpu.CompilerParams(vmem_limit_bytes=56 * 2**20),
        name="finish",
    )(rows_sum, total)
    return (
        grad_rows,
        taps_sum,
        res_sum,
        rate_sum,
        skip_sum.reshape(256),
    )


def solution(mesh):
    in_specs = (
        P("fsdp", "ctx", None),
        P("fsdp", "ctx", None),
        P(None, "fsdp"),
        P(None, "fsdp"),
        P(None, "fsdp"),
        P("fsdp"),
        P("fsdp", None, None),
        P("fsdp", None, None),
    )
    out_specs = (
        P("fsdp", "ctx", None),
        P(None, "fsdp"),
        P(None, "fsdp"),
        P(None, "fsdp"),
        P("fsdp"),
    )
    return jax.shard_map(
        per_device, mesh=mesh, in_specs=in_specs, out_specs=out_specs, check_vma=False
    )
```

```python
import math

import jax
import jax.numpy as jnp
from jax import lax
from jax.experimental import pallas as pl
from jax.experimental.pallas import tpu as pltpu
from jax.sharding import PartitionSpec as P

MESH = pl.DeviceIdType.MESH
F32 = jnp.float32
BF16 = jnp.bfloat16
MODES = 16
LANES = 128
STEPS = 16
OWNERS = 16
ROWS = 88
MODAL = 64
REST = ROWS - MODAL
WIDTH = 8
AHEAD = 4
STAGE1, STAGE2, STAGE3, STAGE4, STAGE5 = 1, 5, 8, 12, 13
MAIN = STAGE5 + 1
TURNS = MAIN + OWNERS
VMEM = pl.BlockSpec(memory_space=pltpu.VMEM)
ANY = pl.BlockSpec(memory_space=pl.ANY)


def remote(src, dst, send, recv, ctx, fsdp):
    return pltpu.make_async_remote_copy(
        src_ref=src, dst_ref=dst, send_sem=send, recv_sem=recv,
        device_id=(ctx, fsdp), device_id_type=MESH,
    )


def greet(ctx, fsdp):
    pl.semaphore_signal(
        pltpu.get_barrier_semaphore(), inc=1, device_id=(ctx, fsdp), device_id_type=MESH
    )


def spread(row):
    return jnp.broadcast_to(row, (8, LANES))


def spread_rows(rows):
    return jnp.broadcast_to(rows[:, None, :], (rows.shape[0], 8, LANES))


def sublane():
    return lax.broadcasted_iota(jnp.int32, (8, LANES), 0)


def row_sum(x):
    return jnp.sum(x, axis=0, keepdims=True)


def tree(terms):
    count = terms.shape[0]
    while count > 1:
        count //= 2
        terms = terms[:count] + terms[count:]
    return terms[0]


def tap_place(section, group, j):
    unit = section * 32 + group
    return unit // 6, pl.ds(MODAL + 6 * j + unit % 6, 1)


def own_rows(group, first, count):
    base = (group % 2) * MODES
    if count % 8 == 0:
        base = pl.multiple_of(base, MODES)
    return group // 2, pl.ds(base + first, count)


def lanes_of(unit, count=1):
    return pl.ds(pl.multiple_of(unit * LANES, LANES), count * LANES)


def local_pass(group, rows, cot, gath, prev, xs, X, F, U, G, C, ends, starts, e_all, s_all, weights):
    sub = sublane()
    top = sub == 0
    feat = []
    for q in range(3):
        unit = q * 32 + group
        xs[...] = rows[0, :, lanes_of(unit)].astype(F32)
        for i in range(STEPS):
            X[group, q, 2 + i] = xs[pl.ds(i, 8, stride=STEPS), :]
        near = spread(prev[pl.ds(96 + unit, 1), :])
        far = spread(prev[pl.ds(unit, 1), :])
        X[group, q, 1] = jnp.where(top, near, pltpu.roll(X[group, q, 17], 1, 0))
        X[group, q, 0] = jnp.where(top, far, pltpu.roll(X[group, q, 16], 1, 0))
        t = [spread(gath[tap_place(q, group, j)]) for j in range(3)]
        feat.append(t[0] * X[group, q, 2:18] + t[1] * X[group, q, 1:17] + t[2] * X[group, q, 0:16])
        if q:
            F[group, q - 1] = feat[q]
    xs[...] = cot[0, :, lanes_of(group)].astype(F32)
    for i in range(STEPS):
        C[group, i] = xs[pl.ds(i, 8, stride=STEPS), :]
    U[group] = feat[1] * feat[2]
    G[group] = C[group] * feat[0]
    rate = gath[own_rows(group, 32, MODES)]
    weights[0] = jnp.exp(-rate)
    weights[1] = jnp.exp(-16.0 * rate)
    weights[2] = jnp.exp(-32.0 * rate)
    weights[3] = jnp.exp(-64.0 * rate)
    d = spread_rows(weights[0])
    e = jnp.broadcast_to(U[group, 0], (MODES, 8, LANES))
    b = jnp.broadcast_to(G[group, 15], (MODES, 8, LANES))
    for i in range(1, STEPS):
        e = d * e + U[group, i]
        b = d * b + G[group, 15 - i]
    for power, shift in ((1, 1), (2, 2), (3, 4)):
        w = spread_rows(weights[power])
        e = e + jnp.where(sub >= shift, w, 0.0) * pltpu.roll(e, shift, 1)
        b = b + jnp.where(sub < 8 - shift, w, 0.0) * pltpu.roll(b, 8 - shift, 1)
    ends[group] = e
    starts[group] = b
    for n in range(MODES):
        e_all[own_rows(group, n, 1)] = e[n, 7:8]
        s_all[own_rows(group, n, 1)] = b[n, 0:1]


def main_pass(group, edge, gath, nxt, xs, X, F, U, G, C, ends, starts, e_all, e_prior, s_prior,
              grads, hist, filt, back, GB, weights):
    sub = sublane()
    scale = 1.0 / math.sqrt(16 * 2048)
    whole = own_rows(group, 0, MODES)
    rate = gath[own_rows(group, 32, MODES)]
    res = gath[whole]
    decay = jnp.exp(-rate)
    weights[0] = decay
    blocks = sub.astype(F32) * -16.0
    blocks_back = (7 - sub).astype(F32) * -16.0
    for base in range(0, MODES, WIDTH):
        some = slice(base, base + WIDTH)
        here = own_rows(group, base, WIDTH)
        d = spread_rows(weights[0, some])
        r = spread_rows(gath[here])
        speed = spread_rows(gath[own_rows(group, 32 + base, WIDTH)])
        state = jnp.where(sub > 0, pltpu.roll(ends[group, some], 1, 1), 0.0)
        state = state + jnp.exp(speed * blocks) * spread_rows(e_prior[here])
        leave = jnp.where(sub < 7, pltpu.roll(starts[group, some], 7, 1), 0.0)
        leave = leave + jnp.exp(speed * blocks_back) * spread_rows(s_prior[here])
        hist[0] = state
        res_sum = jnp.zeros((WIDTH, 8, LANES), F32)
        rate_sum = res_sum
        for i in range(STEPS):
            state = d * state + U[group, i]
            if i + 1 < STEPS:
                hist[i + 1] = state
            res_sum = res_sum + G[group, i] * state
            total = tree(r * state)
            filt[i] = total if base == 0 else filt[i] + total
        for i in range(STEPS - 1, -1, -1):
            leave = d * leave + G[group, i]
            rate_sum = rate_sum + leave * hist[i]
            total = tree(r * leave)
            back[i] = total if base == 0 else back[i] + total
        grads[here] = jnp.sum(res_sum, axis=1) * scale
        grads[own_rows(group, 32 + base, WIDTH)] = (
            jnp.sum(rate_sum, axis=1) * (weights[0, some] * gath[here]) * -scale
        )
    skip_at = (group // 2, pl.ds(82 + group % 2, 1))
    skip_row = gath[skip_at]
    skip = spread(skip_row)

    taps = [[gath[tap_place(q, group, t)] for t in range(3)] for q in range(3)]
    after = []
    for q in range(3):
        unit = q * 32 + group
        x = [X[group, q, 16, 7:8], X[group, q, 17, 7:8],
             nxt[pl.ds(unit, 1), :], nxt[pl.ds(96 + unit, 1), :]]
        after.append([taps[q][0] * x[t] + taps[q][1] * x[t - 1] + taps[q][2] * x[t - 2] for t in (2, 3)])
    next_cot = [nxt[pl.ds(192 + t * 32 + group, 1), :] for t in range(2)]
    next_mixed = [after[1][t] * after[2][t] for t in range(2)]
    next_grad = [next_cot[t] * after[0][t] for t in range(2)]
    state0 = decay * (e_all[whole] + jnp.exp(rate * -128.0) * e_prior[whole]) + next_mixed[0]
    state1 = decay * state0 + next_mixed[1]
    back0 = s_prior[whole]
    back1 = (back0 - next_grad[0]) * jnp.exp(rate)
    follow = [[], [], []]
    for t, (s, b) in enumerate(((state0, back0), (state1, back1))):
        filtered = row_sum(res * s) + skip_row * next_mixed[t]
        mixed = row_sum(res * b) + skip_row * next_grad[t]
        follow[0].append(next_cot[t] * filtered)
        follow[1].append(mixed * after[2][t])
        follow[2].append(mixed * after[1][t])

    u, g = U[group], G[group]
    grads[skip_at] = row_sum(jnp.sum(u * g, axis=0)) * scale
    mixed = back[...] + skip * g
    GB[group, 0, 0:16] = C[group] * (filt[...] + skip * u)
    GB[group, 1, 0:16] = mixed * F[group, 1]
    GB[group, 2, 0:16] = mixed * F[group, 0]
    for q in range(3):
        for k in range(2):
            row = jnp.where(edge, 0.0, follow[q][k])
            GB[group, q, 16 + k] = jnp.where(sub == 7, spread(row), pltpu.roll(GB[group, q, k], 7, 0))
        grad = GB[group, q, 0:16]
        for k in range(3):
            terms = X[group, q, 2 - k : 18 - k] * grad
            grads[tap_place(q, group, k)] = row_sum(jnp.sum(terms, axis=0)) * scale


def rows_pass(group, gath, xs, GB, out):
    for q in range(3):
        t = [spread(gath[tap_place(q, group, k)]) for k in range(3)]
        y = t[0] * GB[group, q, 0:16] + t[1] * GB[group, q, 1:17] + t[2] * GB[group, q, 2:18]
        for i in range(STEPS):
            xs[pl.ds(i, 8, stride=STEPS), :] = y[i]
        out[0, :, lanes_of(q * 32 + group)] = xs[...].astype(BF16)


def kernel(rows_hbm, cot_hbm, taps, residues, rates, skip, before_hbm, after_hbm,
           rows_out, result,
           rows, cot, before, after, out, gath, grads, prev, nxt, tail_f, head_f, tail_b, head_b, prev_b, next_b,
           xs, X, F, U, G, C, ends, starts, e_all, s_all, e_prior, s_prior, hist, filt, back, GB, weights,
           first, second, third, whole, last, agg, chip, begin, inner, span,
           by_y, by_z, relay, rest_y, rest_z, rest_sum, modal_x, modal_across, rest_x, rest_across,
           mine, other,
           in_sem, out_sem, halo_s, halo_r, rest_s, rest_r, modal_s, modal_r, hand_s, hand_r,
           s1, r1, s2, r2, s3, r3, s4, r4, s5, r5,
           ys, yr, zs, zr, rys, ryr, rzs, rzr, mxs, mxr, mas, mar, rxs, rxr, ras, rar, end_s, end_r):
    p = lax.axis_index("ctx")
    f = lax.axis_index("fsdp")
    c, h, x = p % 2, (p // 2) % 2, p // 4
    partner = p + 1 - 2 * c
    across = p + 2 - 4 * h
    resident = h == c
    n = jnp.where(c == 1, x, 3 - x)
    sign = jnp.where(c == 1, 4, -4)
    edge = p == 15
    y, z = f // 4, f % 4
    z_peers = [y * 4 + (z + k) % 4 for k in range(1, 4)]
    y_peers = [(y + k) % 4 * 4 + z for k in range(1, 4)]

    def owner_at(k):
        turn_z = (k // 4 + 1) % 4
        turn_y = (k + k // 12) % 4
        return (y + turn_y) % 4 * 4 + (z + turn_z) % 4

    def local_at(k):
        return owner_at((k + 15) % 16)

    load_rows = pltpu.make_async_copy(rows_hbm, rows, in_sem.at[0])
    load_cot = pltpu.make_async_copy(cot_hbm, cot, in_sem.at[1])
    load_before = pltpu.make_async_copy(before_hbm, before, in_sem.at[2])
    load_after = pltpu.make_async_copy(after_hbm, after, in_sem.at[3])
    for load in (load_rows, load_cot, load_before, load_after):
        load.start()
    for peer in z_peers + y_peers:
        greet(p, peer)
    for step in range(1, 4):
        greet((p + 4 * step) % 16, f)
    greet(across, f)
    greet(partner, f)
    greet((p + 15 + 2 * c) % 16, f)

    for b in range(2):
        cols = slice(LANES * b, LANES * (b + 1))
        gath[f, 16 * b : 16 * (b + 1), :] = residues[:, cols]
        gath[f, 32 + 16 * b : 48 + 16 * b, :] = rates[:, cols]
        gath[f, 82 + b : 83 + b, :] = skip[:, cols]
    for j in range(3):
        for b in range(6):
            row = MODAL + 6 * j + b
            gath[f, row : row + 1, :] = taps[j : j + 1, LANES * b : LANES * (b + 1)]
    gath[f, 84:88, :] = jnp.zeros((4, LANES), F32)
    for o in range(OWNERS):
        grads[o, 84:88, :] = jnp.zeros((4, LANES), F32)

    pl.semaphore_wait(pltpu.get_barrier_semaphore(), 12)

    def rest_copy(k, owner, to):
        block = gath.at[owner, pl.ds(MODAL, REST)]
        return remote(block, block, rest_s.at[k], rest_r.at[owner], p, to)

    part = pl.multiple_of(32 - 32 * c, 32)
    part_other = pl.multiple_of(32 * c, 32)

    def modal_copy(k, owner, to):
        block = gath.at[owner, pl.ds(part, 32)]
        return remote(block, block, modal_s.at[k], modal_r.at[owner], p, to)

    def hand_copy(owner, rows_from):
        block = gath.at[owner, pl.ds(rows_from, 32)]
        return remote(block, block, hand_s.at[owner], hand_r.at[owner], partner, f)

    for make in (rest_copy, modal_copy):
        for k, peer in enumerate(z_peers + y_peers):
            make(k, f, peer).start()

    for load in (load_rows, load_cot, load_before, load_after):
        load.wait()

    def edges(unit, _):
        end = rows[0, 112:128, lanes_of(unit)].astype(F32)
        tail_f[pl.ds(unit, 1), :] = end[14:15]
        tail_f[pl.ds(96 + unit, 1), :] = end[15:16]
        start = rows[0, 0:16, lanes_of(unit)].astype(F32)
        head_f[pl.ds(unit, 1), :] = start[0:1]
        head_f[pl.ds(96 + unit, 1), :] = start[1:2]
        return 0

    def edges_cot(unit, _):
        start = cot[0, 0:16, lanes_of(unit)].astype(F32)
        head_f[pl.ds(192 + unit, 1), :] = start[0:1]
        head_f[pl.ds(224 + unit, 1), :] = start[1:2]
        return 0

    lax.fori_loop(0, 96, edges, 0, unroll=4)
    lax.fori_loop(0, 32, edges_cot, 0, unroll=4)
    tail_b[...] = tail_f[...].astype(BF16)
    head_b[...] = head_f[...].astype(BF16)

    right = remote(tail_b, prev_b, halo_s.at[0], halo_r.at[0], p + 1, f)
    left = remote(head_b, next_b, halo_s.at[1], halo_r.at[1], p - 1, f)

    @pl.when(p < 15)
    def _():
        right.start()

    @pl.when(p > 0)
    def _():
        left.start()

    for make in (rest_copy, modal_copy):
        for k, owner in enumerate(z_peers):
            make(0, owner, f).wait_recv()
            for j, peer in enumerate(y_peers):
                make(6 + 3 * k + j, owner, peer).start()

    @pl.when(p > 0)
    def _():
        right.wait_recv()
        prev[...] = prev_b[...].astype(F32)

    @pl.when(p == 0)
    def _():
        prev[...] = jnp.zeros_like(prev)

    @pl.when(p < 15)
    def _():
        left.wait_recv()
        nxt[...] = next_b[...].astype(F32)

    @pl.when(p == 15)
    def _():
        nxt[...] = jnp.zeros_like(nxt)

    for k in range(4):
        for peer in y_peers:
            rest_copy(0, peer // 4 * 4 + (z + k) % 4, f).wait_recv()

    def hand_on(owner):
        @pl.when(owner // 4 != y)
        def _():
            modal_copy(0, owner, f).wait_recv()
        hand_copy(owner, part).start()

    for k in range(1, 1 + AHEAD):
        hand_on(local_at(k))

    def copy1(o, ref):
        return remote(ref.at[o], first.at[o], s1.at[o], r1.at[o], partner, f)

    def copy2(o):
        return remote(agg.at[o], second.at[o], s2.at[o], r2.at[o], across, f)

    def copy3(o, j):
        return remote(chip.at[o], third.at[j - 1, o], s3.at[j - 1, o], r3.at[j - 1, o], p + sign * j, f)

    def copy4(o):
        return remote(begin.at[o], whole.at[o], s4.at[o], r4.at[o], across, f)

    def copy5(o, ref):
        return remote(ref.at[o], last.at[o], s5.at[o], r5.at[o], partner, f)

    def decay(o, power):
        value = span[o]
        for _ in range(power // 2):
            value = value * value
        return value

    def stage1(o):
        copy1(o, e_all).wait_recv()
        span[o] = jnp.exp(gath[o, 32:64, :] * -128.0)
        own = jnp.where(c == 1, e_all[o], s_all[o])
        agg[o] = own + decay(o, 1) * first[o]

        @pl.when(jnp.logical_not(resident))
        def _():
            copy2(o).start()

    def stage2(o):
        @pl.when(resident)
        def _():
            copy2(o).wait_recv()
            chip[o] = agg[o] + decay(o, 2) * second[o]
            for j in range(1, 4):
                @pl.when(n + j < 4)
                def _():
                    copy3(o, j).start()

    def own_prior(o, value):
        @pl.when(c == 1)
        def _():
            e_prior[o] = value

        @pl.when(c == 0)
        def _():
            s_prior[o] = value

    def stage3(o):
        @pl.when(resident)
        def _():
            for b in range(2):
                cols = lanes_of(2 * o + b)
                begin[o, 16 * b : 16 * (b + 1), :] = jnp.where(c == 1, before[0, :, cols], after[0, :, cols])
            four = decay(o, 4)
            for j in range(3, 0, -1):
                @pl.when(n >= j)
                def _():
                    copy3(o, j).wait_recv()
                    begin[o] = third[j - 1, o] + four * begin[o]
            copy4(o).start()
            inner[o] = decay(o, 2) * begin[o] + second[o]
            copy5(o, inner).start()
            own_prior(o, decay(o, 1) * inner[o] + first[o])

    def stage4(o):
        @pl.when(jnp.logical_not(resident))
        def _():
            copy4(o).wait_recv()
            copy5(o, whole).start()
            own_prior(o, decay(o, 1) * whole[o] + first[o])

    def stage5(o):
        copy5(o, whole).wait_recv()

        @pl.when(c == 1)
        def _():
            s_prior[o] = last[o]

        @pl.when(c == 0)
        def _():
            e_prior[o] = last[o]

    def share_copy(owner, source, to):
        return remote(grads.at[owner, pl.ds(0, MODAL)], by_y.at[owner % 4, source],
                      ys.at[owner], yr.at[owner % 4, source], p, to)

    def relay_copy(to_z, from_z):
        return remote(relay.at[to_z], by_z.at[from_z], zs.at[to_z], zr.at[from_z], p, y * 4 + to_z)

    def gather_y(owner):
        for k in range(1, 4):
            share_copy(owner, (y + k) % 4, f).wait_recv()
        by_y[owner % 4, y] = grads[owner, 0:MODAL]
        return jnp.sum(by_y[owner % 4], axis=0)

    def relay_one(to_z):
        relay[to_z] = gather_y(y * 4 + to_z)
        relay_copy(to_z, z).start()

    def write_rows(begin_group, end_group):
        def one(group, _):
            rows_pass(group, gath, xs, GB, out)
            return 0

        lax.fori_loop(begin_group, end_group, one, 0)

    def turn(t, _):
        @pl.when(t < OWNERS)
        def _():
            @pl.when(t + AHEAD + 1 < OWNERS)
            def _():
                hand_on(local_at(t + AHEAD + 1))
            o = local_at(t)

            @pl.when(t > 0)
            def _():
                hand_copy(o, part_other).wait_recv()

            def one(j, _):
                local_pass(2 * o + j, rows, cot, gath, prev, xs, X, F, U, G, C, ends, starts,
                           e_all, s_all, weights)
                return 0

            lax.fori_loop(0, 2, one, 0)

            @pl.when(c == 0)
            def _():
                copy1(o, e_all).start()

            @pl.when(c == 1)
            def _():
                copy1(o, s_all).start()

        for stage, lag in ((stage5, STAGE5), (stage4, STAGE4), (stage3, STAGE3), (stage2, STAGE2),
                           (stage1, STAGE1)):
            @pl.when(jnp.logical_and(t >= lag, t < lag + OWNERS))
            def _():
                stage(local_at(t - lag))

        @pl.when(t >= MAIN)
        def _():
            o = owner_at(t - MAIN)

            def one(j, _):
                main_pass(2 * o + j, edge, gath, nxt, xs, X, F, U, G, C, ends, starts, e_all,
                          e_prior, s_prior, grads, hist, filt, back, GB, weights)
                return 0

            lax.fori_loop(0, 2, one, 0)

            @pl.when(o // 4 != y)
            def _():
                share_copy(o, y, o // 4 * 4 + z).start()

        for k in range(1, 4):
            @pl.when(t == MAIN + 4 * k + 1)
            def _():
                relay_one((z + k) % 4)

        return 0

    lax.fori_loop(0, TURNS, turn, 0)

    def rest_to_y(to_y, from_y):
        return remote(grads.at[pl.ds(4 * to_y, 4), pl.ds(MODAL, REST)], rest_y.at[from_y],
                      rys.at[to_y], ryr.at[from_y], p, to_y * 4 + z)

    def rest_to_z(to_z, from_z):
        return remote(rest_sum.at[to_z], rest_z.at[from_z], rzs.at[to_z], rzr.at[from_z], p, y * 4 + to_z)

    def over_x(ref, send, recv, k, slot):
        return remote(ref.at[slot], ref.at[slot], send.at[k], recv.at[slot], (p + 4 * k) % 16, f)

    def over_across(ref, send, recv, slot):
        return remote(ref.at[slot], ref.at[slot], send, recv, across, f)

    for k in range(1, 4):
        rest_to_y((y + k) % 4, y).start()
    write_rows(0, 10)
    total = gather_y(f)
    for k in range(1, 4):
        relay_copy(z, (z + k) % 4).wait_recv()
    by_z[z] = total
    modal_x[x] = jnp.sum(by_z[...], axis=0)
    for k in range(1, 4):
        over_x(modal_x, mxs, mxr, k, x).start()

    rest_y[y] = grads[pl.ds(4 * y, 4), MODAL:ROWS, :]
    for k in range(1, 4):
        rest_to_y(y, (y + k) % 4).wait_recv()
    rest_sum[...] = jnp.sum(rest_y[...], axis=0)
    for k in range(1, 4):
        rest_to_z((z + k) % 4, z).start()
    write_rows(10, 22)

    for k in range(1, 4):
        over_x(modal_x, mxs, mxr, k, (x + k) % 4).wait_recv()
    modal_across[h] = jnp.sum(modal_x[...], axis=0)
    over_across(modal_across, mas, mar, h).start()

    rest_z[z] = rest_sum[z]
    for k in range(1, 4):
        rest_to_z(z, (z + k) % 4).wait_recv()
    rest_x[x] = jnp.sum(rest_z[...], axis=0)
    for k in range(1, 4):
        over_x(rest_x, rxs, rxr, k, x).start()
    write_rows(22, 32)
    store = pltpu.make_async_copy(out, rows_out, out_sem)
    store.start()

    over_across(modal_across, mas, mar, 1 - h).wait_recv()
    mine[0:MODAL] = modal_across[0] + modal_across[1]

    for k in range(1, 4):
        over_x(rest_x, rxs, rxr, k, (x + k) % 4).wait_recv()
    rest_across[h] = jnp.sum(rest_x[...], axis=0)
    over_across(rest_across, ras, rar, h).start()
    over_across(rest_across, ras, rar, 1 - h).wait_recv()
    mine[MODAL:ROWS] = rest_across[0] + rest_across[1]
    end = remote(mine, other, end_s, end_r, partner, f)
    end.start()

    @pl.when(p < 15)
    def _():
        right.wait_send()

    @pl.when(p > 0)
    def _():
        left.wait_send()

    for k in range(15):
        rest_copy(k, f, f).wait_send()
        modal_copy(k, f, f).wait_send()
    for k in range(1, 4):
        relay_copy((z + k) % 4, z).wait_send()
        rest_to_y((y + k) % 4, y).wait_send()
        rest_to_z((z + k) % 4, z).wait_send()
        over_x(modal_x, mxs, mxr, k, x).wait_send()
        over_x(rest_x, rxs, rxr, k, x).wait_send()
    over_across(modal_across, mas, mar, h).wait_send()
    over_across(rest_across, ras, rar, h).wait_send()

    def drain(o, _):
        copy1(o, e_all).wait_send()

        @pl.when(resident)
        def _():
            for j in range(1, 4):
                @pl.when(n + j < 4)
                def _():
                    copy3(o, j).wait_send()
            copy4(o).wait_send()

        @pl.when(jnp.logical_not(resident))
        def _():
            copy2(o).wait_send()
        copy5(o, whole).wait_send()

        @pl.when(o != f)
        def _():
            hand_copy(o, part).wait_send()

        @pl.when(o // 4 != y)
        def _():
            share_copy(o, y, f).wait_send()
        return 0

    lax.fori_loop(0, OWNERS, drain, 0)
    store.wait()
    end.wait_recv()
    result[...] = mine[...] + other[...]
    end.wait_send()


def finish(rows_in, mine, rows_out, taps_out, res_out, rate_out, skip_out, held, load_sem, store_sem):
    def piece(k):
        return slice(None), slice(16 * k, 16 * (k + 1))

    loads = [pltpu.make_async_copy(rows_in.at[piece(k)], held.at[piece(k)], load_sem.at[k]) for k in range(8)]
    stores = [pltpu.make_async_copy(held.at[piece(k)], rows_out.at[piece(k)], store_sem.at[k]) for k in range(8)]
    for load in loads:
        load.start()
    for b in range(2):
        cols = slice(LANES * b, LANES * (b + 1))
        res_out[:, cols] = mine[16 * b : 16 * (b + 1), :]
        rate_out[:, cols] = mine[32 + 16 * b : 48 + 16 * b, :]
        skip_out[:, cols] = mine[82 + b : 83 + b, :]
    for j in range(3):
        for b in range(6):
            row = MODAL + 6 * j + b
            taps_out[j : j + 1, LANES * b : LANES * (b + 1)] = mine[row : row + 1, :]
    for load, store in zip(loads, stores):
        load.wait()
        store.start()
    for store in stores:
        store.wait()

def shape(*dims, dtype=F32):
    return jax.ShapeDtypeStruct(dims, dtype)


def per_device(rows_in, cotangent, taps, residues, rates, skip, state_before, adjoint_after):
    def buf(*dims, dtype=F32):
        return pltpu.VMEM(dims, dtype)

    def sems(*dims):
        return pltpu.SemaphoreType.DMA(dims)

    vec = buf(32, STEPS, 8, LANES)
    small = buf(OWNERS, 2 * MODES, LANES)
    each = [sems(16), sems(16)]
    four = [sems(4), sems(4)]
    one = [sems(), sems()]
    rows_sum, total = pl.pallas_call(
        kernel,
        out_shape=(shape(1, 128, 12288, dtype=BF16), shape(ROWS, LANES)),
        in_specs=[ANY, ANY] + [VMEM] * 4 + [ANY, ANY],
        out_specs=(ANY, VMEM),
        scratch_shapes=[
            buf(1, 128, 12288, dtype=BF16), buf(1, 128, 4096, dtype=BF16), buf(1, MODES, 4096), buf(1, MODES, 4096),
            buf(1, 128, 12288, dtype=BF16),
            buf(OWNERS, ROWS, LANES), buf(OWNERS, ROWS, LANES), buf(192, LANES), buf(256, LANES),
            buf(192, LANES), buf(256, LANES), buf(192, LANES, dtype=BF16), buf(256, LANES, dtype=BF16),
            buf(192, LANES, dtype=BF16), buf(256, LANES, dtype=BF16),
            buf(128, LANES), buf(32, 3, 18, 8, LANES), buf(32, 2, STEPS, 8, LANES), vec, vec, vec,
            vec, vec, small, small, small, small, buf(STEPS, WIDTH, 8, LANES),
            buf(STEPS, 8, LANES), buf(STEPS, 8, LANES), buf(32, 3, 18, 8, LANES), buf(4, MODES, LANES),
            small, small, buf(3, OWNERS, 2 * MODES, LANES), small, small, small, small, small, small, small,
            buf(4, 4, MODAL, LANES), buf(4, MODAL, LANES), buf(4, MODAL, LANES),
            buf(4, 4, REST, LANES), buf(4, REST, LANES), buf(4, REST, LANES),
            buf(4, MODAL, LANES), buf(2, MODAL, LANES), buf(4, REST, LANES), buf(2, REST, LANES),
            buf(ROWS, LANES), buf(ROWS, LANES),
            sems(4), sems(), sems(2), sems(2), *each, *each, *each,
            *each, *each, sems(3, 16), sems(3, 16), *each, *each,
            sems(16), sems(4, 4), *four, *four, *four, *four, *one, *four, *one, *one,
        ],
        compiler_params=pltpu.CompilerParams(
            collective_id=1, has_side_effects=True, vmem_limit_bytes=56 * 2**20
        ),
        cost_estimate=pl.CostEstimate(flops=10**8, bytes_accessed=8 * 2**20, transcendentals=10**5),
        name="hyena",
    )(rows_in, cotangent, taps, residues, rates, skip[None, :], state_before, adjoint_after)
    grad_rows, taps_sum, res_sum, rate_sum, skip_sum = pl.pallas_call(
        finish,
        out_shape=(shape(1, 128, 12288, dtype=BF16), shape(3, 768), shape(16, 256), shape(16, 256),
                   shape(1, 256)),
        in_specs=[ANY, VMEM],
        out_specs=(ANY,) + (VMEM,) * 4,
        scratch_shapes=[buf(1, 128, 12288, dtype=BF16), sems(8), sems(8)],
        compiler_params=pltpu.CompilerParams(vmem_limit_bytes=56 * 2**20),
        name="finish",
    )(rows_sum, total)
    return (
        grad_rows,
        taps_sum,
        res_sum,
        rate_sum,
        skip_sum.reshape(256),
    )


def solution(mesh):
    in_specs = (
        P("fsdp", "ctx", None),
        P("fsdp", "ctx", None),
        P(None, "fsdp"),
        P(None, "fsdp"),
        P(None, "fsdp"),
        P("fsdp"),
        P("fsdp", None, None),
        P("fsdp", None, None),
    )
    out_specs = (
        P("fsdp", "ctx", None),
        P(None, "fsdp"),
        P(None, "fsdp"),
        P(None, "fsdp"),
        P("fsdp"),
    )
    return jax.shard_map(
        per_device, mesh=mesh, in_specs=in_specs, out_specs=out_specs, check_vma=False
    )
```

```python
import math

import jax
import jax.numpy as jnp
from jax import lax
from jax.experimental import pallas as pl
from jax.experimental.pallas import tpu as pltpu
from jax.sharding import PartitionSpec as P

MESH = pl.DeviceIdType.MESH
F32 = jnp.float32
BF16 = jnp.bfloat16
MODES = 16
LANES = 128
STEPS = 16
OWNERS = 16
ROWS = 88
MODAL = 64
REST = ROWS - MODAL
WIDTH = 8
AHEAD = 4
STAGE1, STAGE2, STAGE3, STAGE4, STAGE5 = 1, 5, 8, 12, 13
MAIN = STAGE5 + 1
TURNS = MAIN + OWNERS
VMEM = pl.BlockSpec(memory_space=pltpu.VMEM)
ANY = pl.BlockSpec(memory_space=pl.ANY)


def remote(src, dst, send, recv, ctx, fsdp):
    return pltpu.make_async_remote_copy(
        src_ref=src, dst_ref=dst, send_sem=send, recv_sem=recv,
        device_id=(ctx, fsdp), device_id_type=MESH,
    )


def greet(ctx, fsdp):
    pl.semaphore_signal(
        pltpu.get_barrier_semaphore(), inc=1, device_id=(ctx, fsdp), device_id_type=MESH
    )


def spread(row):
    return jnp.broadcast_to(row, (8, LANES))


def spread_rows(rows):
    return jnp.broadcast_to(rows[:, None, :], (rows.shape[0], 8, LANES))


def sublane():
    return lax.broadcasted_iota(jnp.int32, (8, LANES), 0)


def row_sum(x):
    return jnp.sum(x, axis=0, keepdims=True)


def tree(terms):
    count = terms.shape[0]
    while count > 1:
        count //= 2
        terms = terms[:count] + terms[count:]
    return terms[0]


def tap_place(section, group, j):
    unit = section * 32 + group
    return unit // 6, pl.ds(MODAL + 6 * j + unit % 6, 1)


def own_rows(group, first, count):
    base = (group % 2) * MODES
    if count % 8 == 0:
        base = pl.multiple_of(base, MODES)
    return group // 2, pl.ds(base + first, count)


def lanes_of(unit, count=1):
    return pl.ds(pl.multiple_of(unit * LANES, LANES), count * LANES)


def local_pass(group, rows, cot, gath, prev, xs, X, F, U, G, C, ends, starts, e_all, s_all, weights):
    sub = sublane()
    top = sub == 0
    feat = []
    for q in range(3):
        unit = q * 32 + group
        xs[...] = rows[0, :, lanes_of(unit)].astype(F32)
        for i in range(STEPS):
            X[group, q, 2 + i] = xs[pl.ds(i, 8, stride=STEPS), :]
        near = spread(prev[pl.ds(96 + unit, 1), :])
        far = spread(prev[pl.ds(unit, 1), :])
        X[group, q, 1] = jnp.where(top, near, pltpu.roll(X[group, q, 17], 1, 0))
        X[group, q, 0] = jnp.where(top, far, pltpu.roll(X[group, q, 16], 1, 0))
        t = [spread(gath[tap_place(q, group, j)]) for j in range(3)]
        feat.append(t[0] * X[group, q, 2:18] + t[1] * X[group, q, 1:17] + t[2] * X[group, q, 0:16])
        if q:
            F[group, q - 1] = feat[q]
    xs[...] = cot[0, :, lanes_of(group)].astype(F32)
    for i in range(STEPS):
        C[group, i] = xs[pl.ds(i, 8, stride=STEPS), :]
    U[group] = feat[1] * feat[2]
    G[group] = C[group] * feat[0]
    rate = gath[own_rows(group, 32, MODES)]
    weights[0] = jnp.exp(-rate)
    weights[1] = jnp.exp(-16.0 * rate)
    weights[2] = jnp.exp(-32.0 * rate)
    weights[3] = jnp.exp(-64.0 * rate)
    d = spread_rows(weights[0])
    e = jnp.broadcast_to(U[group, 0], (MODES, 8, LANES))
    b = jnp.broadcast_to(G[group, 15], (MODES, 8, LANES))
    for i in range(1, STEPS):
        e = d * e + U[group, i]
        b = d * b + G[group, 15 - i]
    for power, shift in ((1, 1), (2, 2), (3, 4)):
        w = spread_rows(weights[power])
        e = e + jnp.where(sub >= shift, w, 0.0) * pltpu.roll(e, shift, 1)
        b = b + jnp.where(sub < 8 - shift, w, 0.0) * pltpu.roll(b, 8 - shift, 1)
    ends[group] = e
    starts[group] = b
    for n in range(MODES):
        e_all[own_rows(group, n, 1)] = e[n, 7:8]
        s_all[own_rows(group, n, 1)] = b[n, 0:1]


def main_pass(group, edge, gath, nxt, xs, X, F, U, G, C, ends, starts, e_all, e_prior, s_prior,
              grads, hist, filt, back, GB, weights):
    sub = sublane()
    scale = 1.0 / math.sqrt(16 * 2048)
    whole = own_rows(group, 0, MODES)
    rate = gath[own_rows(group, 32, MODES)]
    res = gath[whole]
    decay = jnp.exp(-rate)
    weights[0] = decay
    blocks = sub.astype(F32) * -16.0
    blocks_back = (7 - sub).astype(F32) * -16.0
    for base in range(0, MODES, WIDTH):
        some = slice(base, base + WIDTH)
        here = own_rows(group, base, WIDTH)
        d = spread_rows(weights[0, some])
        r = spread_rows(gath[here])
        speed = spread_rows(gath[own_rows(group, 32 + base, WIDTH)])
        state = jnp.where(sub > 0, pltpu.roll(ends[group, some], 1, 1), 0.0)
        state = state + jnp.exp(speed * blocks) * spread_rows(e_prior[here])
        leave = jnp.where(sub < 7, pltpu.roll(starts[group, some], 7, 1), 0.0)
        leave = leave + jnp.exp(speed * blocks_back) * spread_rows(s_prior[here])
        hist[0] = state
        res_sum = jnp.zeros((WIDTH, 8, LANES), F32)
        rate_sum = res_sum
        for i in range(STEPS):
            state = d * state + U[group, i]
            if i + 1 < STEPS:
                hist[i + 1] = state
            res_sum = res_sum + G[group, i] * state
            total = tree(r * state)
            filt[i] = total if base == 0 else filt[i] + total
        for i in range(STEPS - 1, -1, -1):
            leave = d * leave + G[group, i]
            rate_sum = rate_sum + leave * hist[i]
            total = tree(r * leave)
            back[i] = total if base == 0 else back[i] + total
        grads[here] = jnp.sum(res_sum, axis=1) * scale
        grads[own_rows(group, 32 + base, WIDTH)] = (
            jnp.sum(rate_sum, axis=1) * (weights[0, some] * gath[here]) * -scale
        )
    skip_at = (group // 2, pl.ds(82 + group % 2, 1))
    skip_row = gath[skip_at]
    skip = spread(skip_row)

    taps = [[gath[tap_place(q, group, t)] for t in range(3)] for q in range(3)]
    after = []
    for q in range(3):
        unit = q * 32 + group
        x = [X[group, q, 16, 7:8], X[group, q, 17, 7:8],
             nxt[pl.ds(unit, 1), :], nxt[pl.ds(96 + unit, 1), :]]
        after.append([taps[q][0] * x[t] + taps[q][1] * x[t - 1] + taps[q][2] * x[t - 2] for t in (2, 3)])
    next_cot = [nxt[pl.ds(192 + t * 32 + group, 1), :] for t in range(2)]
    next_mixed = [after[1][t] * after[2][t] for t in range(2)]
    next_grad = [next_cot[t] * after[0][t] for t in range(2)]
    state0 = decay * (e_all[whole] + jnp.exp(rate * -128.0) * e_prior[whole]) + next_mixed[0]
    state1 = decay * state0 + next_mixed[1]
    back0 = s_prior[whole]
    back1 = (back0 - next_grad[0]) * jnp.exp(rate)
    follow = [[], [], []]
    for t, (s, b) in enumerate(((state0, back0), (state1, back1))):
        filtered = row_sum(res * s) + skip_row * next_mixed[t]
        mixed = row_sum(res * b) + skip_row * next_grad[t]
        follow[0].append(next_cot[t] * filtered)
        follow[1].append(mixed * after[2][t])
        follow[2].append(mixed * after[1][t])

    u, g = U[group], G[group]
    grads[skip_at] = row_sum(jnp.sum(u * g, axis=0)) * scale
    mixed = back[...] + skip * g
    GB[group, 0, 0:16] = C[group] * (filt[...] + skip * u)
    GB[group, 1, 0:16] = mixed * F[group, 1]
    GB[group, 2, 0:16] = mixed * F[group, 0]
    for q in range(3):
        for k in range(2):
            row = jnp.where(edge, 0.0, follow[q][k])
            GB[group, q, 16 + k] = jnp.where(sub == 7, spread(row), pltpu.roll(GB[group, q, k], 7, 0))
        grad = GB[group, q, 0:16]
        for k in range(3):
            terms = X[group, q, 2 - k : 18 - k] * grad
            grads[tap_place(q, group, k)] = row_sum(jnp.sum(terms, axis=0)) * scale


def rows_pass(group, gath, xs, GB, out):
    for q in range(3):
        t = [spread(gath[tap_place(q, group, k)]) for k in range(3)]
        y = t[0] * GB[group, q, 0:16] + t[1] * GB[group, q, 1:17] + t[2] * GB[group, q, 2:18]
        for i in range(STEPS):
            xs[pl.ds(i, 8, stride=STEPS), :] = y[i]
        out[0, :, lanes_of(q * 32 + group)] = xs[...].astype(BF16)


def kernel(rows_hbm, cot_hbm, taps, residues, rates, skip, before_hbm, after_hbm,
           out, result,
           rows, cot, before, after, gath, grads, prev, nxt, tail_f, head_f, tail_b, head_b, prev_b, next_b,
           xs, X, F, U, G, C, ends, starts, e_all, s_all, e_prior, s_prior, hist, filt, back, GB, weights,
           first, second, third, whole, last, agg, chip, begin, inner, span,
           by_y, by_z, relay, rest_y, rest_z, rest_sum, modal_x, modal_across, rest_x, rest_across,
           mine, other,
           in_sem, halo_s, halo_r, rest_s, rest_r, modal_s, modal_r, hand_s, hand_r,
           s1, r1, s2, r2, s3, r3, s4, r4, s5, r5,
           ys, yr, zs, zr, rys, ryr, rzs, rzr, mxs, mxr, mas, mar, rxs, rxr, ras, rar, end_s, end_r):
    p = lax.axis_index("ctx")
    f = lax.axis_index("fsdp")
    c, h, x = p % 2, (p // 2) % 2, p // 4
    partner = p + 1 - 2 * c
    across = p + 2 - 4 * h
    resident = h == c
    n = jnp.where(c == 1, x, 3 - x)
    sign = jnp.where(c == 1, 4, -4)
    edge = p == 15
    y, z = f // 4, f % 4
    z_peers = [y * 4 + (z + k) % 4 for k in range(1, 4)]
    y_peers = [(y + k) % 4 * 4 + z for k in range(1, 4)]

    def owner_at(k):
        turn_z = (k // 4 + 1) % 4
        turn_y = (k + k // 12) % 4
        return (y + turn_y) % 4 * 4 + (z + turn_z) % 4

    def local_at(k):
        return owner_at((k + 15) % 16)

    load_rows = pltpu.make_async_copy(rows_hbm, rows, in_sem.at[0])
    load_cot = pltpu.make_async_copy(cot_hbm, cot, in_sem.at[1])
    load_before = pltpu.make_async_copy(before_hbm, before, in_sem.at[2])
    load_after = pltpu.make_async_copy(after_hbm, after, in_sem.at[3])
    for load in (load_rows, load_cot, load_before, load_after):
        load.start()
    for peer in z_peers + y_peers:
        greet(p, peer)
    for step in range(1, 4):
        greet((p + 4 * step) % 16, f)
    greet(across, f)
    greet(partner, f)
    greet((p + 15 + 2 * c) % 16, f)

    for b in range(2):
        cols = slice(LANES * b, LANES * (b + 1))
        gath[f, 16 * b : 16 * (b + 1), :] = residues[:, cols]
        gath[f, 32 + 16 * b : 48 + 16 * b, :] = rates[:, cols]
        gath[f, 82 + b : 83 + b, :] = skip[:, cols]
    for j in range(3):
        for b in range(6):
            row = MODAL + 6 * j + b
            gath[f, row : row + 1, :] = taps[j : j + 1, LANES * b : LANES * (b + 1)]
    gath[f, 84:88, :] = jnp.zeros((4, LANES), F32)
    for o in range(OWNERS):
        grads[o, 84:88, :] = jnp.zeros((4, LANES), F32)

    pl.semaphore_wait(pltpu.get_barrier_semaphore(), 12)

    def rest_copy(k, owner, to):
        block = gath.at[owner, pl.ds(MODAL, REST)]
        return remote(block, block, rest_s.at[k], rest_r.at[owner], p, to)

    part = pl.multiple_of(32 - 32 * c, 32)
    part_other = pl.multiple_of(32 * c, 32)

    def modal_copy(k, owner, to):
        block = gath.at[owner, pl.ds(part, 32)]
        return remote(block, block, modal_s.at[k], modal_r.at[owner], p, to)

    def hand_copy(owner, rows_from):
        block = gath.at[owner, pl.ds(rows_from, 32)]
        return remote(block, block, hand_s.at[owner], hand_r.at[owner], partner, f)

    for make in (rest_copy, modal_copy):
        for k, peer in enumerate(z_peers + y_peers):
            make(k, f, peer).start()

    for load in (load_rows, load_cot, load_before, load_after):
        load.wait()

    def edges(unit, _):
        end = rows[0, 112:128, lanes_of(unit)].astype(F32)
        tail_f[pl.ds(unit, 1), :] = end[14:15]
        tail_f[pl.ds(96 + unit, 1), :] = end[15:16]
        start = rows[0, 0:16, lanes_of(unit)].astype(F32)
        head_f[pl.ds(unit, 1), :] = start[0:1]
        head_f[pl.ds(96 + unit, 1), :] = start[1:2]
        return 0

    def edges_cot(unit, _):
        start = cot[0, 0:16, lanes_of(unit)].astype(F32)
        head_f[pl.ds(192 + unit, 1), :] = start[0:1]
        head_f[pl.ds(224 + unit, 1), :] = start[1:2]
        return 0

    lax.fori_loop(0, 96, edges, 0, unroll=4)
    lax.fori_loop(0, 32, edges_cot, 0, unroll=4)
    tail_b[...] = tail_f[...].astype(BF16)
    head_b[...] = head_f[...].astype(BF16)

    right = remote(tail_b, prev_b, halo_s.at[0], halo_r.at[0], p + 1, f)
    left = remote(head_b, next_b, halo_s.at[1], halo_r.at[1], p - 1, f)

    @pl.when(p < 15)
    def _():
        right.start()

    @pl.when(p > 0)
    def _():
        left.start()

    for make in (rest_copy, modal_copy):
        for k, owner in enumerate(z_peers):
            make(0, owner, f).wait_recv()
            for j, peer in enumerate(y_peers):
                make(6 + 3 * k + j, owner, peer).start()

    @pl.when(p > 0)
    def _():
        right.wait_recv()
        prev[...] = prev_b[...].astype(F32)

    @pl.when(p == 0)
    def _():
        prev[...] = jnp.zeros_like(prev)

    @pl.when(p < 15)
    def _():
        left.wait_recv()
        nxt[...] = next_b[...].astype(F32)

    @pl.when(p == 15)
    def _():
        nxt[...] = jnp.zeros_like(nxt)

    for k in range(4):
        for peer in y_peers:
            rest_copy(0, peer // 4 * 4 + (z + k) % 4, f).wait_recv()

    def hand_on(owner):
        @pl.when(owner // 4 != y)
        def _():
            modal_copy(0, owner, f).wait_recv()
        hand_copy(owner, part).start()

    for k in range(1, 1 + AHEAD):
        hand_on(local_at(k))

    def copy1(o, ref):
        return remote(ref.at[o], first.at[o], s1.at[o], r1.at[o], partner, f)

    def copy2(o):
        return remote(agg.at[o], second.at[o], s2.at[o], r2.at[o], across, f)

    def copy3(o, j):
        return remote(chip.at[o], third.at[j - 1, o], s3.at[j - 1, o], r3.at[j - 1, o], p + sign * j, f)

    def copy4(o):
        return remote(begin.at[o], whole.at[o], s4.at[o], r4.at[o], across, f)

    def copy5(o, ref):
        return remote(ref.at[o], last.at[o], s5.at[o], r5.at[o], partner, f)

    def decay(o, power):
        value = span[o]
        for _ in range(power // 2):
            value = value * value
        return value

    def stage1(o):
        copy1(o, e_all).wait_recv()
        span[o] = jnp.exp(gath[o, 32:64, :] * -128.0)
        own = jnp.where(c == 1, e_all[o], s_all[o])
        agg[o] = own + decay(o, 1) * first[o]

        @pl.when(jnp.logical_not(resident))
        def _():
            copy2(o).start()

    def stage2(o):
        @pl.when(resident)
        def _():
            copy2(o).wait_recv()
            chip[o] = agg[o] + decay(o, 2) * second[o]
            for j in range(1, 4):
                @pl.when(n + j < 4)
                def _():
                    copy3(o, j).start()

    def own_prior(o, value):
        @pl.when(c == 1)
        def _():
            e_prior[o] = value

        @pl.when(c == 0)
        def _():
            s_prior[o] = value

    def stage3(o):
        @pl.when(resident)
        def _():
            for b in range(2):
                cols = lanes_of(2 * o + b)
                begin[o, 16 * b : 16 * (b + 1), :] = jnp.where(c == 1, before[0, :, cols], after[0, :, cols])
            four = decay(o, 4)
            for j in range(3, 0, -1):
                @pl.when(n >= j)
                def _():
                    copy3(o, j).wait_recv()
                    begin[o] = third[j - 1, o] + four * begin[o]
            copy4(o).start()
            inner[o] = decay(o, 2) * begin[o] + second[o]
            copy5(o, inner).start()
            own_prior(o, decay(o, 1) * inner[o] + first[o])

    def stage4(o):
        @pl.when(jnp.logical_not(resident))
        def _():
            copy4(o).wait_recv()
            copy5(o, whole).start()
            own_prior(o, decay(o, 1) * whole[o] + first[o])

    def stage5(o):
        copy5(o, whole).wait_recv()

        @pl.when(c == 1)
        def _():
            s_prior[o] = last[o]

        @pl.when(c == 0)
        def _():
            e_prior[o] = last[o]

    def share_copy(owner, source, to):
        return remote(grads.at[owner, pl.ds(0, MODAL)], by_y.at[owner % 4, source],
                      ys.at[owner], yr.at[owner % 4, source], p, to)

    def relay_copy(to_z, from_z):
        return remote(relay.at[to_z], by_z.at[from_z], zs.at[to_z], zr.at[from_z], p, y * 4 + to_z)

    def gather_y(owner):
        for k in range(1, 4):
            share_copy(owner, (y + k) % 4, f).wait_recv()
        by_y[owner % 4, y] = grads[owner, 0:MODAL]
        return jnp.sum(by_y[owner % 4], axis=0)

    def relay_one(to_z):
        relay[to_z] = gather_y(y * 4 + to_z)
        relay_copy(to_z, z).start()

    def write_rows(begin_group, end_group):
        def one(group, _):
            rows_pass(group, gath, xs, GB, out)
            return 0

        lax.fori_loop(begin_group, end_group, one, 0)

    def turn(t, _):
        @pl.when(t < OWNERS)
        def _():
            @pl.when(t + AHEAD + 1 < OWNERS)
            def _():
                hand_on(local_at(t + AHEAD + 1))
            o = local_at(t)

            @pl.when(t > 0)
            def _():
                hand_copy(o, part_other).wait_recv()

            def one(j, _):
                local_pass(2 * o + j, rows, cot, gath, prev, xs, X, F, U, G, C, ends, starts,
                           e_all, s_all, weights)
                return 0

            lax.fori_loop(0, 2, one, 0)

            @pl.when(c == 0)
            def _():
                copy1(o, e_all).start()

            @pl.when(c == 1)
            def _():
                copy1(o, s_all).start()

        for stage, lag in ((stage5, STAGE5), (stage4, STAGE4), (stage3, STAGE3), (stage2, STAGE2),
                           (stage1, STAGE1)):
            @pl.when(jnp.logical_and(t >= lag, t < lag + OWNERS))
            def _():
                stage(local_at(t - lag))

        @pl.when(t >= MAIN)
        def _():
            o = owner_at(t - MAIN)

            def one(j, _):
                main_pass(2 * o + j, edge, gath, nxt, xs, X, F, U, G, C, ends, starts, e_all,
                          e_prior, s_prior, grads, hist, filt, back, GB, weights)
                return 0

            lax.fori_loop(0, 2, one, 0)

            @pl.when(o // 4 != y)
            def _():
                share_copy(o, y, o // 4 * 4 + z).start()

        for k in range(1, 4):
            @pl.when(t == MAIN + 4 * k + 1)
            def _():
                relay_one((z + k) % 4)

        return 0

    lax.fori_loop(0, TURNS, turn, 0)

    def rest_to_y(to_y, from_y):
        return remote(grads.at[pl.ds(4 * to_y, 4), pl.ds(MODAL, REST)], rest_y.at[from_y],
                      rys.at[to_y], ryr.at[from_y], p, to_y * 4 + z)

    def rest_to_z(to_z, from_z):
        return remote(rest_sum.at[to_z], rest_z.at[from_z], rzs.at[to_z], rzr.at[from_z], p, y * 4 + to_z)

    def over_x(ref, send, recv, k, slot):
        return remote(ref.at[slot], ref.at[slot], send.at[k], recv.at[slot], (p + 4 * k) % 16, f)

    def over_across(ref, send, recv, slot):
        return remote(ref.at[slot], ref.at[slot], send, recv, across, f)

    for k in range(1, 4):
        rest_to_y((y + k) % 4, y).start()
    write_rows(0, 10)
    total = gather_y(f)
    for k in range(1, 4):
        relay_copy(z, (z + k) % 4).wait_recv()
    by_z[z] = total
    modal_x[x] = jnp.sum(by_z[...], axis=0)
    for k in range(1, 4):
        over_x(modal_x, mxs, mxr, k, x).start()

    rest_y[y] = grads[pl.ds(4 * y, 4), MODAL:ROWS, :]
    for k in range(1, 4):
        rest_to_y(y, (y + k) % 4).wait_recv()
    rest_sum[...] = jnp.sum(rest_y[...], axis=0)
    for k in range(1, 4):
        rest_to_z((z + k) % 4, z).start()
    write_rows(10, 22)

    for k in range(1, 4):
        over_x(modal_x, mxs, mxr, k, (x + k) % 4).wait_recv()
    modal_across[h] = jnp.sum(modal_x[...], axis=0)
    over_across(modal_across, mas, mar, h).start()

    rest_z[z] = rest_sum[z]
    for k in range(1, 4):
        rest_to_z(z, (z + k) % 4).wait_recv()
    rest_x[x] = jnp.sum(rest_z[...], axis=0)
    for k in range(1, 4):
        over_x(rest_x, rxs, rxr, k, x).start()
    write_rows(22, 32)

    over_across(modal_across, mas, mar, 1 - h).wait_recv()
    mine[0:MODAL] = modal_across[0] + modal_across[1]

    for k in range(1, 4):
        over_x(rest_x, rxs, rxr, k, (x + k) % 4).wait_recv()
    rest_across[h] = jnp.sum(rest_x[...], axis=0)
    over_across(rest_across, ras, rar, h).start()
    over_across(rest_across, ras, rar, 1 - h).wait_recv()
    mine[MODAL:ROWS] = rest_across[0] + rest_across[1]
    end = remote(mine, other, end_s, end_r, partner, f)
    end.start()

    @pl.when(p < 15)
    def _():
        right.wait_send()

    @pl.when(p > 0)
    def _():
        left.wait_send()

    for k in range(15):
        rest_copy(k, f, f).wait_send()
        modal_copy(k, f, f).wait_send()
    for k in range(1, 4):
        relay_copy((z + k) % 4, z).wait_send()
        rest_to_y((y + k) % 4, y).wait_send()
        rest_to_z((z + k) % 4, z).wait_send()
        over_x(modal_x, mxs, mxr, k, x).wait_send()
        over_x(rest_x, rxs, rxr, k, x).wait_send()
    over_across(modal_across, mas, mar, h).wait_send()
    over_across(rest_across, ras, rar, h).wait_send()

    def drain(o, _):
        copy1(o, e_all).wait_send()

        @pl.when(resident)
        def _():
            for j in range(1, 4):
                @pl.when(n + j < 4)
                def _():
                    copy3(o, j).wait_send()
            copy4(o).wait_send()

        @pl.when(jnp.logical_not(resident))
        def _():
            copy2(o).wait_send()
        copy5(o, whole).wait_send()

        @pl.when(o != f)
        def _():
            hand_copy(o, part).wait_send()

        @pl.when(o // 4 != y)
        def _():
            share_copy(o, y, f).wait_send()
        return 0

    lax.fori_loop(0, OWNERS, drain, 0)
    end.wait_recv()
    result[...] = mine[...] + other[...]
    end.wait_send()


def finish(rows_in, mine, rows_out, taps_out, res_out, rate_out, skip_out, store_sem):
    def piece(k):
        return slice(None), slice(16 * k, 16 * (k + 1))

    stores = [pltpu.make_async_copy(rows_in.at[piece(k)], rows_out.at[piece(k)], store_sem.at[k]) for k in range(8)]
    for store in stores:
        store.start()
    for b in range(2):
        cols = slice(LANES * b, LANES * (b + 1))
        res_out[:, cols] = mine[16 * b : 16 * (b + 1), :]
        rate_out[:, cols] = mine[32 + 16 * b : 48 + 16 * b, :]
        skip_out[:, cols] = mine[82 + b : 83 + b, :]
    for j in range(3):
        for b in range(6):
            row = MODAL + 6 * j + b
            taps_out[j : j + 1, LANES * b : LANES * (b + 1)] = mine[row : row + 1, :]
    for store in stores:
        store.wait()

def shape(*dims, dtype=F32):
    return jax.ShapeDtypeStruct(dims, dtype)


def per_device(rows_in, cotangent, taps, residues, rates, skip, state_before, adjoint_after):
    def buf(*dims, dtype=F32):
        return pltpu.VMEM(dims, dtype)

    def sems(*dims):
        return pltpu.SemaphoreType.DMA(dims)

    vec = buf(32, STEPS, 8, LANES)
    small = buf(OWNERS, 2 * MODES, LANES)
    each = [sems(16), sems(16)]
    four = [sems(4), sems(4)]
    one = [sems(), sems()]
    rows_sum, total = pl.pallas_call(
        kernel,
        out_shape=(pltpu.VMEM((1, 128, 12288), BF16), pltpu.VMEM((ROWS, LANES), F32)),
        in_specs=[ANY, ANY] + [VMEM] * 4 + [ANY, ANY],
        out_specs=(VMEM, VMEM),
        scratch_shapes=[
            buf(1, 128, 12288, dtype=BF16), buf(1, 128, 4096, dtype=BF16), buf(1, MODES, 4096), buf(1, MODES, 4096),
            buf(OWNERS, ROWS, LANES), buf(OWNERS, ROWS, LANES), buf(192, LANES), buf(256, LANES),
            buf(192, LANES), buf(256, LANES), buf(192, LANES, dtype=BF16), buf(256, LANES, dtype=BF16),
            buf(192, LANES, dtype=BF16), buf(256, LANES, dtype=BF16),
            buf(128, LANES), buf(32, 3, 18, 8, LANES), buf(32, 2, STEPS, 8, LANES), vec, vec, vec,
            vec, vec, small, small, small, small, buf(STEPS, WIDTH, 8, LANES),
            buf(STEPS, 8, LANES), buf(STEPS, 8, LANES), buf(32, 3, 18, 8, LANES), buf(4, MODES, LANES),
            small, small, buf(3, OWNERS, 2 * MODES, LANES), small, small, small, small, small, small, small,
            buf(4, 4, MODAL, LANES), buf(4, MODAL, LANES), buf(4, MODAL, LANES),
            buf(4, 4, REST, LANES), buf(4, REST, LANES), buf(4, REST, LANES),
            buf(4, MODAL, LANES), buf(2, MODAL, LANES), buf(4, REST, LANES), buf(2, REST, LANES),
            buf(ROWS, LANES), buf(ROWS, LANES),
            sems(4), sems(2), sems(2), *each, *each, *each,
            *each, *each, sems(3, 16), sems(3, 16), *each, *each,
            sems(16), sems(4, 4), *four, *four, *four, *four, *one, *four, *one, *one,
        ],
        compiler_params=pltpu.CompilerParams(
            collective_id=1, has_side_effects=True, vmem_limit_bytes=56 * 2**20
        ),
        cost_estimate=pl.CostEstimate(flops=10**8, bytes_accessed=8 * 2**20, transcendentals=10**5),
        name="hyena",
    )(rows_in, cotangent, taps, residues, rates, skip[None, :], state_before, adjoint_after)
    grad_rows, taps_sum, res_sum, rate_sum, skip_sum = pl.pallas_call(
        finish,
        out_shape=(shape(1, 128, 12288, dtype=BF16), shape(3, 768), shape(16, 256), shape(16, 256),
                   shape(1, 256)),
        in_specs=[VMEM, VMEM],
        out_specs=(ANY,) + (VMEM,) * 4,
        scratch_shapes=[sems(8)],
        compiler_params=pltpu.CompilerParams(vmem_limit_bytes=16 * 2**20),
        name="finish",
    )(rows_sum, total)
    return (
        grad_rows,
        taps_sum,
        res_sum,
        rate_sum,
        skip_sum.reshape(256),
    )


def solution(mesh):
    in_specs = (
        P("fsdp", "ctx", None),
        P("fsdp", "ctx", None),
        P(None, "fsdp"),
        P(None, "fsdp"),
        P(None, "fsdp"),
        P("fsdp"),
        P("fsdp", None, None),
        P("fsdp", None, None),
    )
    out_specs = (
        P("fsdp", "ctx", None),
        P(None, "fsdp"),
        P(None, "fsdp"),
        P(None, "fsdp"),
        P("fsdp"),
    )
    return jax.shard_map(
        per_device, mesh=mesh, in_specs=in_specs, out_specs=out_specs, check_vma=False
    )
```

```python
import math

import jax
import jax.numpy as jnp
from jax import lax
from jax.experimental import pallas as pl
from jax.experimental.pallas import tpu as pltpu
from jax.sharding import PartitionSpec as P

MESH = pl.DeviceIdType.MESH
F32 = jnp.float32
BF16 = jnp.bfloat16
MODES = 16
LANES = 128
STEPS = 16
OWNERS = 16
ROWS = 88
MODAL = 64
REST = ROWS - MODAL
WIDTH = 8
AHEAD = 4
STAGE1, STAGE2, STAGE3, STAGE4, STAGE5 = 1, 5, 8, 12, 13
MAIN = STAGE5 + 1
TURNS = MAIN + OWNERS
VMEM = pl.BlockSpec(memory_space=pltpu.VMEM)
ANY = pl.BlockSpec(memory_space=pl.ANY)


def remote(src, dst, send, recv, ctx, fsdp):
    return pltpu.make_async_remote_copy(
        src_ref=src, dst_ref=dst, send_sem=send, recv_sem=recv,
        device_id=(ctx, fsdp), device_id_type=MESH,
    )


def greet(ctx, fsdp):
    pl.semaphore_signal(
        pltpu.get_barrier_semaphore(), inc=1, device_id=(ctx, fsdp), device_id_type=MESH
    )


def spread(row):
    return jnp.broadcast_to(row, (8, LANES))


def spread_rows(rows):
    return jnp.broadcast_to(rows[:, None, :], (rows.shape[0], 8, LANES))


def sublane():
    return lax.broadcasted_iota(jnp.int32, (8, LANES), 0)


def row_sum(x):
    return jnp.sum(x, axis=0, keepdims=True)


def tree(terms):
    count = terms.shape[0]
    while count > 1:
        count //= 2
        terms = terms[:count] + terms[count:]
    return terms[0]


def tap_place(section, group, j):
    unit = section * 32 + group
    return unit // 6, pl.ds(MODAL + 6 * j + unit % 6, 1)


def own_rows(group, first, count):
    base = (group % 2) * MODES
    if count % 8 == 0:
        base = pl.multiple_of(base, MODES)
    return group // 2, pl.ds(base + first, count)


def lanes_of(unit, count=1):
    return pl.ds(pl.multiple_of(unit * LANES, LANES), count * LANES)


def local_pass(group, rows, cot, gath, prev, xs, X, F, U, G, C, ends, starts, e_all, s_all, weights):
    sub = sublane()
    top = sub == 0
    feat = []
    for q in range(3):
        unit = q * 32 + group
        xs[...] = rows[0, :, lanes_of(unit)].astype(F32)
        for i in range(STEPS):
            X[group, q, 2 + i] = xs[pl.ds(i, 8, stride=STEPS), :]
        near = spread(prev[pl.ds(96 + unit, 1), :])
        far = spread(prev[pl.ds(unit, 1), :])
        X[group, q, 1] = jnp.where(top, near, pltpu.roll(X[group, q, 17], 1, 0))
        X[group, q, 0] = jnp.where(top, far, pltpu.roll(X[group, q, 16], 1, 0))
        t = [spread(gath[tap_place(q, group, j)]) for j in range(3)]
        feat.append(t[0] * X[group, q, 2:18] + t[1] * X[group, q, 1:17] + t[2] * X[group, q, 0:16])
        if q:
            F[group, q - 1] = feat[q]
    xs[...] = cot[0, :, lanes_of(group)].astype(F32)
    for i in range(STEPS):
        C[group, i] = xs[pl.ds(i, 8, stride=STEPS), :]
    U[group] = feat[1] * feat[2]
    G[group] = C[group] * feat[0]
    rate = gath[own_rows(group, 32, MODES)]
    weights[0] = jnp.exp(-rate)
    weights[1] = jnp.exp(-16.0 * rate)
    weights[2] = jnp.exp(-32.0 * rate)
    weights[3] = jnp.exp(-64.0 * rate)
    d = spread_rows(weights[0])
    e = jnp.broadcast_to(U[group, 0], (MODES, 8, LANES))
    b = jnp.broadcast_to(G[group, 15], (MODES, 8, LANES))
    for i in range(1, STEPS):
        e = d * e + U[group, i]
        b = d * b + G[group, 15 - i]
    for power, shift in ((1, 1), (2, 2), (3, 4)):
        w = spread_rows(weights[power])
        e = e + jnp.where(sub >= shift, w, 0.0) * pltpu.roll(e, shift, 1)
        b = b + jnp.where(sub < 8 - shift, w, 0.0) * pltpu.roll(b, 8 - shift, 1)
    ends[group] = e
    starts[group] = b
    for n in range(MODES):
        e_all[own_rows(group, n, 1)] = e[n, 7:8]
        s_all[own_rows(group, n, 1)] = b[n, 0:1]


def main_pass(group, edge, gath, nxt, xs, X, F, U, G, C, ends, starts, e_all, e_prior, s_prior,
              grads, hist, filt, back, GB, weights):
    sub = sublane()
    scale = 1.0 / math.sqrt(16 * 2048)
    whole = own_rows(group, 0, MODES)
    rate = gath[own_rows(group, 32, MODES)]
    res = gath[whole]
    decay = jnp.exp(-rate)
    weights[0] = decay
    blocks = sub.astype(F32) * -16.0
    blocks_back = (7 - sub).astype(F32) * -16.0
    for base in range(0, MODES, WIDTH):
        some = slice(base, base + WIDTH)
        here = own_rows(group, base, WIDTH)
        d = spread_rows(weights[0, some])
        r = spread_rows(gath[here])
        speed = spread_rows(gath[own_rows(group, 32 + base, WIDTH)])
        state = jnp.where(sub > 0, pltpu.roll(ends[group, some], 1, 1), 0.0)
        state = state + jnp.exp(speed * blocks) * spread_rows(e_prior[here])
        leave = jnp.where(sub < 7, pltpu.roll(starts[group, some], 7, 1), 0.0)
        leave = leave + jnp.exp(speed * blocks_back) * spread_rows(s_prior[here])
        hist[0] = state
        res_sum = jnp.zeros((WIDTH, 8, LANES), F32)
        rate_sum = res_sum
        for i in range(STEPS):
            state = d * state + U[group, i]
            if i + 1 < STEPS:
                hist[i + 1] = state
            res_sum = res_sum + G[group, i] * state
            total = tree(r * state)
            filt[i] = total if base == 0 else filt[i] + total
        for i in range(STEPS - 1, -1, -1):
            leave = d * leave + G[group, i]
            rate_sum = rate_sum + leave * hist[i]
            total = tree(r * leave)
            back[i] = total if base == 0 else back[i] + total
        grads[here] = jnp.sum(res_sum, axis=1) * scale
        grads[own_rows(group, 32 + base, WIDTH)] = (
            jnp.sum(rate_sum, axis=1) * (weights[0, some] * gath[here]) * -scale
        )
    skip_at = (group // 2, pl.ds(82 + group % 2, 1))
    skip_row = gath[skip_at]
    skip = spread(skip_row)

    taps = [[gath[tap_place(q, group, t)] for t in range(3)] for q in range(3)]
    after = []
    for q in range(3):
        unit = q * 32 + group
        x = [X[group, q, 16, 7:8], X[group, q, 17, 7:8],
             nxt[pl.ds(unit, 1), :], nxt[pl.ds(96 + unit, 1), :]]
        after.append([taps[q][0] * x[t] + taps[q][1] * x[t - 1] + taps[q][2] * x[t - 2] for t in (2, 3)])
    next_cot = [nxt[pl.ds(192 + t * 32 + group, 1), :] for t in range(2)]
    next_mixed = [after[1][t] * after[2][t] for t in range(2)]
    next_grad = [next_cot[t] * after[0][t] for t in range(2)]
    state0 = decay * (e_all[whole] + jnp.exp(rate * -128.0) * e_prior[whole]) + next_mixed[0]
    state1 = decay * state0 + next_mixed[1]
    back0 = s_prior[whole]
    back1 = (back0 - next_grad[0]) * jnp.exp(rate)
    follow = [[], [], []]
    for t, (s, b) in enumerate(((state0, back0), (state1, back1))):
        filtered = row_sum(res * s) + skip_row * next_mixed[t]
        mixed = row_sum(res * b) + skip_row * next_grad[t]
        follow[0].append(next_cot[t] * filtered)
        follow[1].append(mixed * after[2][t])
        follow[2].append(mixed * after[1][t])

    u, g = U[group], G[group]
    grads[skip_at] = row_sum(jnp.sum(u * g, axis=0)) * scale
    mixed = back[...] + skip * g
    GB[group, 0, 0:16] = C[group] * (filt[...] + skip * u)
    GB[group, 1, 0:16] = mixed * F[group, 1]
    GB[group, 2, 0:16] = mixed * F[group, 0]
    for q in range(3):
        for k in range(2):
            row = jnp.where(edge, 0.0, follow[q][k])
            GB[group, q, 16 + k] = jnp.where(sub == 7, spread(row), pltpu.roll(GB[group, q, k], 7, 0))
        grad = GB[group, q, 0:16]
        for k in range(3):
            terms = X[group, q, 2 - k : 18 - k] * grad
            grads[tap_place(q, group, k)] = row_sum(jnp.sum(terms, axis=0)) * scale


def rows_pass(group, gath, xs, GB, out):
    for q in range(3):
        t = [spread(gath[tap_place(q, group, k)]) for k in range(3)]
        y = t[0] * GB[group, q, 0:16] + t[1] * GB[group, q, 1:17] + t[2] * GB[group, q, 2:18]
        for i in range(STEPS):
            xs[pl.ds(i, 8, stride=STEPS), :] = y[i]
        out[0, :, lanes_of(q * 32 + group)] = xs[...].astype(BF16)


def kernel(rows_hbm, cot_hbm, taps, residues, rates, skip, before_hbm, after_hbm,
           out, result,
           rows, cot, before, after, gath, grads, prev, nxt, tail_f, head_f, tail_b, head_b, prev_b, next_b,
           xs, X, F, U, G, C, ends, starts, e_all, s_all, e_prior, s_prior, hist, filt, back, GB, weights,
           first, second, third, whole, last, agg, chip, begin, inner, span,
           by_y, by_z, relay, rest_y, rest_z, rest_sum, modal_x, modal_across, rest_x, rest_across,
           mine, other,
           in_sem, halo_s, halo_r, rest_s, rest_r, modal_s, modal_r, hand_s, hand_r,
           s1, r1, s2, r2, s3, r3, s4, r4, s5, r5,
           ys, yr, zs, zr, rys, ryr, rzs, rzr, mxs, mxr, mas, mar, rxs, rxr, ras, rar, end_s, end_r):
    p = lax.axis_index("ctx")
    f = lax.axis_index("fsdp")
    c, h, x = p % 2, (p // 2) % 2, p // 4
    partner = p + 1 - 2 * c
    across = p + 2 - 4 * h
    resident = h == c
    n = jnp.where(c == 1, x, 3 - x)
    sign = jnp.where(c == 1, 4, -4)
    edge = p == 15
    y, z = f // 4, f % 4
    z_peers = [y * 4 + (z + k) % 4 for k in range(1, 4)]
    y_peers = [(y + k) % 4 * 4 + z for k in range(1, 4)]

    def owner_at(k):
        turn_z = (k // 4 + 1) % 4
        turn_y = (k + k // 12) % 4
        return (y + turn_y) % 4 * 4 + (z + turn_z) % 4

    def local_at(k):
        return owner_at((k + 15) % 16)

    load_rows = pltpu.make_async_copy(rows_hbm, rows, in_sem.at[0])
    load_cot = pltpu.make_async_copy(cot_hbm, cot, in_sem.at[1])
    load_before = pltpu.make_async_copy(before_hbm, before, in_sem.at[2])
    load_after = pltpu.make_async_copy(after_hbm, after, in_sem.at[3])
    for load in (load_rows, load_cot, load_before, load_after):
        load.start()
    for peer in z_peers + y_peers:
        greet(p, peer)
    for step in range(1, 4):
        greet((p + 4 * step) % 16, f)
    greet(across, f)
    greet(partner, f)
    greet((p + 15 + 2 * c) % 16, f)

    for b in range(2):
        cols = slice(LANES * b, LANES * (b + 1))
        gath[f, 16 * b : 16 * (b + 1), :] = residues[:, cols]
        gath[f, 32 + 16 * b : 48 + 16 * b, :] = rates[:, cols]
        gath[f, 82 + b : 83 + b, :] = skip[:, cols]
    for j in range(3):
        for b in range(6):
            row = MODAL + 6 * j + b
            gath[f, row : row + 1, :] = taps[j : j + 1, LANES * b : LANES * (b + 1)]
    gath[f, 84:88, :] = jnp.zeros((4, LANES), F32)
    for o in range(OWNERS):
        grads[o, 84:88, :] = jnp.zeros((4, LANES), F32)

    pl.semaphore_wait(pltpu.get_barrier_semaphore(), 12)

    def rest_copy(k, owner, to):
        block = gath.at[owner, pl.ds(MODAL, REST)]
        return remote(block, block, rest_s.at[k], rest_r.at[owner], p, to)

    part = pl.multiple_of(32 - 32 * c, 32)
    part_other = pl.multiple_of(32 * c, 32)

    def modal_copy(k, owner, to):
        block = gath.at[owner, pl.ds(part, 32)]
        return remote(block, block, modal_s.at[k], modal_r.at[owner], p, to)

    def hand_copy(owner, rows_from):
        block = gath.at[owner, pl.ds(rows_from, 32)]
        return remote(block, block, hand_s.at[owner], hand_r.at[owner], partner, f)

    for make in (rest_copy, modal_copy):
        for k, peer in enumerate(z_peers + y_peers):
            make(k, f, peer).start()

    for load in (load_rows, load_cot, load_before, load_after):
        load.wait()

    def edges(unit, _):
        end = rows[0, 112:128, lanes_of(unit)].astype(F32)
        tail_f[pl.ds(unit, 1), :] = end[14:15]
        tail_f[pl.ds(96 + unit, 1), :] = end[15:16]
        start = rows[0, 0:16, lanes_of(unit)].astype(F32)
        head_f[pl.ds(unit, 1), :] = start[0:1]
        head_f[pl.ds(96 + unit, 1), :] = start[1:2]
        return 0

    def edges_cot(unit, _):
        start = cot[0, 0:16, lanes_of(unit)].astype(F32)
        head_f[pl.ds(192 + unit, 1), :] = start[0:1]
        head_f[pl.ds(224 + unit, 1), :] = start[1:2]
        return 0

    lax.fori_loop(0, 96, edges, 0, unroll=4)
    lax.fori_loop(0, 32, edges_cot, 0, unroll=4)
    tail_b[...] = tail_f[...].astype(BF16)
    head_b[...] = head_f[...].astype(BF16)

    right = remote(tail_b, prev_b, halo_s.at[0], halo_r.at[0], p + 1, f)
    left = remote(head_b, next_b, halo_s.at[1], halo_r.at[1], p - 1, f)

    @pl.when(p < 15)
    def _():
        right.start()

    @pl.when(p > 0)
    def _():
        left.start()

    for make in (rest_copy, modal_copy):
        for k, owner in enumerate(z_peers):
            make(0, owner, f).wait_recv()
            for j, peer in enumerate(y_peers):
                make(6 + 3 * k + j, owner, peer).start()

    @pl.when(p > 0)
    def _():
        right.wait_recv()
        prev[...] = prev_b[...].astype(F32)

    @pl.when(p == 0)
    def _():
        prev[...] = jnp.zeros_like(prev)

    @pl.when(p < 15)
    def _():
        left.wait_recv()
        nxt[...] = next_b[...].astype(F32)

    @pl.when(p == 15)
    def _():
        nxt[...] = jnp.zeros_like(nxt)

    for k in range(4):
        for peer in y_peers:
            rest_copy(0, peer // 4 * 4 + (z + k) % 4, f).wait_recv()

    def hand_on(owner):
        @pl.when(owner // 4 != y)
        def _():
            modal_copy(0, owner, f).wait_recv()
        hand_copy(owner, part).start()

    for k in range(1, 1 + AHEAD):
        hand_on(local_at(k))

    def copy1(o, ref):
        return remote(ref.at[o], first.at[o], s1.at[o], r1.at[o], partner, f)

    def copy2(o):
        return remote(agg.at[o], second.at[o], s2.at[o], r2.at[o], across, f)

    def copy3(o, j):
        return remote(chip.at[o], third.at[j - 1, o], s3.at[j - 1, o], r3.at[j - 1, o], p + sign * j, f)

    def copy4(o):
        return remote(begin.at[o], whole.at[o], s4.at[o], r4.at[o], across, f)

    def copy5(o, ref):
        return remote(ref.at[o], last.at[o], s5.at[o], r5.at[o], partner, f)

    def decay(o, power):
        value = span[o]
        for _ in range(power // 2):
            value = value * value
        return value

    def stage1(o):
        copy1(o, e_all).wait_recv()
        span[o] = jnp.exp(gath[o, 32:64, :] * -128.0)
        own = jnp.where(c == 1, e_all[o], s_all[o])
        agg[o] = own + decay(o, 1) * first[o]

        @pl.when(jnp.logical_not(resident))
        def _():
            copy2(o).start()

    def stage2(o):
        @pl.when(resident)
        def _():
            copy2(o).wait_recv()
            chip[o] = agg[o] + decay(o, 2) * second[o]
            for j in range(1, 4):
                @pl.when(n + j < 4)
                def _():
                    copy3(o, j).start()

    def own_prior(o, value):
        @pl.when(c == 1)
        def _():
            e_prior[o] = value

        @pl.when(c == 0)
        def _():
            s_prior[o] = value

    def stage3(o):
        @pl.when(resident)
        def _():
            for b in range(2):
                cols = lanes_of(2 * o + b)
                begin[o, 16 * b : 16 * (b + 1), :] = jnp.where(c == 1, before[0, :, cols], after[0, :, cols])
            four = decay(o, 4)
            for j in range(3, 0, -1):
                @pl.when(n >= j)
                def _():
                    copy3(o, j).wait_recv()
                    begin[o] = third[j - 1, o] + four * begin[o]
            copy4(o).start()
            inner[o] = decay(o, 2) * begin[o] + second[o]
            copy5(o, inner).start()
            own_prior(o, decay(o, 1) * inner[o] + first[o])

    def stage4(o):
        @pl.when(jnp.logical_not(resident))
        def _():
            copy4(o).wait_recv()
            copy5(o, whole).start()
            own_prior(o, decay(o, 1) * whole[o] + first[o])

    def stage5(o):
        copy5(o, whole).wait_recv()

        @pl.when(c == 1)
        def _():
            s_prior[o] = last[o]

        @pl.when(c == 0)
        def _():
            e_prior[o] = last[o]

    def share_copy(owner, source, to):
        return remote(grads.at[owner, pl.ds(0, MODAL)], by_y.at[owner % 4, source],
                      ys.at[owner], yr.at[owner % 4, source], p, to)

    def relay_copy(to_z, from_z):
        return remote(relay.at[to_z], by_z.at[from_z], zs.at[to_z], zr.at[from_z], p, y * 4 + to_z)

    def gather_y(owner):
        for k in range(1, 4):
            share_copy(owner, (y + k) % 4, f).wait_recv()
        by_y[owner % 4, y] = grads[owner, 0:MODAL]
        return jnp.sum(by_y[owner % 4], axis=0)

    def relay_one(to_z):
        relay[to_z] = gather_y(y * 4 + to_z)
        relay_copy(to_z, z).start()

    def write_rows(begin_group, end_group):
        def one(group, _):
            rows_pass(group, gath, xs.at[0], GB, out)
            return 0

        lax.fori_loop(begin_group, end_group, one, 0)

    def turn(t, _):
        @pl.when(t < OWNERS)
        def _():
            @pl.when(t + AHEAD + 1 < OWNERS)
            def _():
                hand_on(local_at(t + AHEAD + 1))
            o = local_at(t)

            @pl.when(t > 0)
            def _():
                hand_copy(o, part_other).wait_recv()

            for j in range(2):
                local_pass(2 * o + j, rows, cot, gath, prev, xs.at[j], X, F, U, G, C, ends, starts,
                           e_all, s_all, weights.at[j])

            @pl.when(c == 0)
            def _():
                copy1(o, e_all).start()

            @pl.when(c == 1)
            def _():
                copy1(o, s_all).start()

        for stage, lag in ((stage5, STAGE5), (stage4, STAGE4), (stage3, STAGE3), (stage2, STAGE2),
                           (stage1, STAGE1)):
            @pl.when(jnp.logical_and(t >= lag, t < lag + OWNERS))
            def _():
                stage(local_at(t - lag))

        @pl.when(t >= MAIN)
        def _():
            o = owner_at(t - MAIN)

            for j in range(2):
                main_pass(2 * o + j, edge, gath, nxt, xs.at[j], X, F, U, G, C, ends, starts, e_all,
                          e_prior, s_prior, grads, hist, filt, back, GB, weights.at[j])

            @pl.when(o // 4 != y)
            def _():
                share_copy(o, y, o // 4 * 4 + z).start()

        for k in range(1, 4):
            @pl.when(t == MAIN + 4 * k + 1)
            def _():
                relay_one((z + k) % 4)

        return 0

    lax.fori_loop(0, TURNS, turn, 0)

    def rest_to_y(to_y, from_y):
        return remote(grads.at[pl.ds(4 * to_y, 4), pl.ds(MODAL, REST)], rest_y.at[from_y],
                      rys.at[to_y], ryr.at[from_y], p, to_y * 4 + z)

    def rest_to_z(to_z, from_z):
        return remote(rest_sum.at[to_z], rest_z.at[from_z], rzs.at[to_z], rzr.at[from_z], p, y * 4 + to_z)

    def over_x(ref, send, recv, k, slot):
        return remote(ref.at[slot], ref.at[slot], send.at[k], recv.at[slot], (p + 4 * k) % 16, f)

    def over_across(ref, send, recv, slot):
        return remote(ref.at[slot], ref.at[slot], send, recv, across, f)

    for k in range(1, 4):
        rest_to_y((y + k) % 4, y).start()
    write_rows(0, 10)
    total = gather_y(f)
    for k in range(1, 4):
        relay_copy(z, (z + k) % 4).wait_recv()
    by_z[z] = total
    modal_x[x] = jnp.sum(by_z[...], axis=0)
    for k in range(1, 4):
        over_x(modal_x, mxs, mxr, k, x).start()

    rest_y[y] = grads[pl.ds(4 * y, 4), MODAL:ROWS, :]
    for k in range(1, 4):
        rest_to_y(y, (y + k) % 4).wait_recv()
    rest_sum[...] = jnp.sum(rest_y[...], axis=0)
    for k in range(1, 4):
        rest_to_z((z + k) % 4, z).start()
    write_rows(10, 22)

    for k in range(1, 4):
        over_x(modal_x, mxs, mxr, k, (x + k) % 4).wait_recv()
    modal_across[h] = jnp.sum(modal_x[...], axis=0)
    over_across(modal_across, mas, mar, h).start()

    rest_z[z] = rest_sum[z]
    for k in range(1, 4):
        rest_to_z(z, (z + k) % 4).wait_recv()
    rest_x[x] = jnp.sum(rest_z[...], axis=0)
    for k in range(1, 4):
        over_x(rest_x, rxs, rxr, k, x).start()
    write_rows(22, 32)

    over_across(modal_across, mas, mar, 1 - h).wait_recv()
    mine[0:MODAL] = modal_across[0] + modal_across[1]

    for k in range(1, 4):
        over_x(rest_x, rxs, rxr, k, (x + k) % 4).wait_recv()
    rest_across[h] = jnp.sum(rest_x[...], axis=0)
    over_across(rest_across, ras, rar, h).start()
    over_across(rest_across, ras, rar, 1 - h).wait_recv()
    mine[MODAL:ROWS] = rest_across[0] + rest_across[1]
    end = remote(mine, other, end_s, end_r, partner, f)
    end.start()

    @pl.when(p < 15)
    def _():
        right.wait_send()

    @pl.when(p > 0)
    def _():
        left.wait_send()

    for k in range(15):
        rest_copy(k, f, f).wait_send()
        modal_copy(k, f, f).wait_send()
    for k in range(1, 4):
        relay_copy((z + k) % 4, z).wait_send()
        rest_to_y((y + k) % 4, y).wait_send()
        rest_to_z((z + k) % 4, z).wait_send()
        over_x(modal_x, mxs, mxr, k, x).wait_send()
        over_x(rest_x, rxs, rxr, k, x).wait_send()
    over_across(modal_across, mas, mar, h).wait_send()
    over_across(rest_across, ras, rar, h).wait_send()

    def drain(o, _):
        copy1(o, e_all).wait_send()

        @pl.when(resident)
        def _():
            for j in range(1, 4):
                @pl.when(n + j < 4)
                def _():
                    copy3(o, j).wait_send()
            copy4(o).wait_send()

        @pl.when(jnp.logical_not(resident))
        def _():
            copy2(o).wait_send()
        copy5(o, whole).wait_send()

        @pl.when(o != f)
        def _():
            hand_copy(o, part).wait_send()

        @pl.when(o // 4 != y)
        def _():
            share_copy(o, y, f).wait_send()
        return 0

    lax.fori_loop(0, OWNERS, drain, 0)
    end.wait_recv()
    result[...] = mine[...] + other[...]
    end.wait_send()


def finish(rows_in, mine, rows_out, taps_out, res_out, rate_out, skip_out, store_sem):
    def piece(k):
        return slice(None), slice(16 * k, 16 * (k + 1))

    stores = [pltpu.make_async_copy(rows_in.at[piece(k)], rows_out.at[piece(k)], store_sem.at[k]) for k in range(8)]
    for store in stores:
        store.start()
    for b in range(2):
        cols = slice(LANES * b, LANES * (b + 1))
        res_out[:, cols] = mine[16 * b : 16 * (b + 1), :]
        rate_out[:, cols] = mine[32 + 16 * b : 48 + 16 * b, :]
        skip_out[:, cols] = mine[82 + b : 83 + b, :]
    for j in range(3):
        for b in range(6):
            row = MODAL + 6 * j + b
            taps_out[j : j + 1, LANES * b : LANES * (b + 1)] = mine[row : row + 1, :]
    for store in stores:
        store.wait()

def shape(*dims, dtype=F32):
    return jax.ShapeDtypeStruct(dims, dtype)


def per_device(rows_in, cotangent, taps, residues, rates, skip, state_before, adjoint_after):
    def buf(*dims, dtype=F32):
        return pltpu.VMEM(dims, dtype)

    def sems(*dims):
        return pltpu.SemaphoreType.DMA(dims)

    vec = buf(32, STEPS, 8, LANES)
    small = buf(OWNERS, 2 * MODES, LANES)
    each = [sems(16), sems(16)]
    four = [sems(4), sems(4)]
    one = [sems(), sems()]
    rows_sum, total = pl.pallas_call(
        kernel,
        out_shape=(pltpu.VMEM((1, 128, 12288), BF16), pltpu.VMEM((ROWS, LANES), F32)),
        in_specs=[ANY, ANY] + [VMEM] * 4 + [ANY, ANY],
        out_specs=(VMEM, VMEM),
        scratch_shapes=[
            buf(1, 128, 12288, dtype=BF16), buf(1, 128, 4096, dtype=BF16), buf(1, MODES, 4096), buf(1, MODES, 4096),
            buf(OWNERS, ROWS, LANES), buf(OWNERS, ROWS, LANES), buf(192, LANES), buf(256, LANES),
            buf(192, LANES), buf(256, LANES), buf(192, LANES, dtype=BF16), buf(256, LANES, dtype=BF16),
            buf(192, LANES, dtype=BF16), buf(256, LANES, dtype=BF16),
            buf(2, 128, LANES), buf(32, 3, 18, 8, LANES), buf(32, 2, STEPS, 8, LANES), vec, vec, vec,
            vec, vec, small, small, small, small, buf(STEPS, WIDTH, 8, LANES),
            buf(STEPS, 8, LANES), buf(STEPS, 8, LANES), buf(32, 3, 18, 8, LANES), buf(2, 4, MODES, LANES),
            small, small, buf(3, OWNERS, 2 * MODES, LANES), small, small, small, small, small, small, small,
            buf(4, 4, MODAL, LANES), buf(4, MODAL, LANES), buf(4, MODAL, LANES),
            buf(4, 4, REST, LANES), buf(4, REST, LANES), buf(4, REST, LANES),
            buf(4, MODAL, LANES), buf(2, MODAL, LANES), buf(4, REST, LANES), buf(2, REST, LANES),
            buf(ROWS, LANES), buf(ROWS, LANES),
            sems(4), sems(2), sems(2), *each, *each, *each,
            *each, *each, sems(3, 16), sems(3, 16), *each, *each,
            sems(16), sems(4, 4), *four, *four, *four, *four, *one, *four, *one, *one,
        ],
        compiler_params=pltpu.CompilerParams(
            collective_id=1, has_side_effects=True, vmem_limit_bytes=56 * 2**20
        ),
        cost_estimate=pl.CostEstimate(flops=10**8, bytes_accessed=8 * 2**20, transcendentals=10**5),
        name="hyena",
    )(rows_in, cotangent, taps, residues, rates, skip[None, :], state_before, adjoint_after)
    grad_rows, taps_sum, res_sum, rate_sum, skip_sum = pl.pallas_call(
        finish,
        out_shape=(shape(1, 128, 12288, dtype=BF16), shape(3, 768), shape(16, 256), shape(16, 256),
                   shape(1, 256)),
        in_specs=[VMEM, VMEM],
        out_specs=(ANY,) + (VMEM,) * 4,
        scratch_shapes=[sems(8)],
        compiler_params=pltpu.CompilerParams(vmem_limit_bytes=16 * 2**20),
        name="finish",
    )(rows_sum, total)
    return (
        grad_rows,
        taps_sum,
        res_sum,
        rate_sum,
        skip_sum.reshape(256),
    )


def solution(mesh):
    in_specs = (
        P("fsdp", "ctx", None),
        P("fsdp", "ctx", None),
        P(None, "fsdp"),
        P(None, "fsdp"),
        P(None, "fsdp"),
        P("fsdp"),
        P("fsdp", None, None),
        P("fsdp", None, None),
    )
    out_specs = (
        P("fsdp", "ctx", None),
        P(None, "fsdp"),
        P(None, "fsdp"),
        P(None, "fsdp"),
        P("fsdp"),
    )
    return jax.shard_map(
        per_device, mesh=mesh, in_specs=in_specs, out_specs=out_specs, check_vma=False
    )
```
